512 devices in a mesh: grp: 64 (over x, z, core), sub: 8 (over y).
Axes of the slice: x: 4, y: 8, z: 8, core: 2. Of those that a mesh axis runs over, the one named last changes fastest.
Arguments:
- dual_coeffs: bfloat16 [32, 196608], P(None, ('grp', 'sub')), may hold values from -6 to 6
- refine_select: int32 [196608], P(('grp', 'sub')), may hold values from 0 to 3
- refine_tiles: bfloat16 [4, 128, 32], replicated, may hold values from -1 to 1
- near_list: int32 [196608, 27], P(('grp', 'sub')), may hold values from -1 to 1151, as said below
- near_tiles: bfloat16 [27, 128, 128], replicated, may hold values from -0.25 to 0.25
- leaf_list: int32 [196608, 32], P(('grp', 'sub')), may hold values from -1 to 1151
- p2m: bfloat16 [169, 128], replicated, may hold values from -0.5 to 0.5
- m2m: bfloat16 [8, 169, 169], replicated, may hold values from -0.15625 to 0.15625
- leaf_m2l: bfloat16 [32, 169, 169], replicated, may hold values from -0.078125 to 0.078125
- coarse_list: int32 [24576, 16], P(('grp', 'sub')), may hold values from -1 to 1151
- coarse_m2l: bfloat16 [16, 169, 169], replicated, may hold values from -0.125 to 0.125
Outputs:
- tested: bfloat16 [32, 196608], P(None, ('grp', 'sub'))
The draws below stay inside these ranges and needn't reach their ends.
Inputs may be any that keep to these rules, and one draw needn't show every extreme that they name: `near_list`: direction 13 of every box but box 0 names the box itself, 384 plus its index within its device.
All inputs are finite; a program needn't handle non-finite values.
Results may differ from the reference program's by a relative error of at most 0.007.
Values may be sent and summed in bfloat16 or wider, within the bound.
No kernel may reach another device: no remote copies, remote signals or barrier semaphores. Data moves between devices by JAX's collectives and lax.ppermute only.
A program may use at most 64 MiB of HBM per device.

```python
import jax
import jax.numpy as jnp

S = 32
SB = 128
Q = 169
RT = 4
NC = 32
NCC = 16
BD = 384
GCB = 384
BOXES = 196608
CBOXES = 24576


def window_lists(key, rows, width, span):
    indices = jax.random.randint(key, (rows, width), 0, span)
    dropped = jax.random.randint(jax.random.fold_in(key, 1), (rows, width), 0, 4)
    indices = jnp.where(dropped == 0, -1, indices)
    indices = indices.at[0, 0].set(span - 1).at[0, 1].set(-1)
    return indices.astype(jnp.int32)


def draw_near_list(key, part):
    key = jax.random.fold_in(key, 11)
    lists = window_lists(key, BOXES, 27, 3 * BD)
    itself = BD + jnp.arange(BOXES, dtype=jnp.int32) % BD
    lists = lists.at[1:, 13].set(itself[1:])
    return lists.astype(jnp.int32)


def draw_leaf_list(key, part):
    key = jax.random.fold_in(key, 12)
    return window_lists(key, BOXES, NC, 3 * BD)


def draw_coarse_list(key, part):
    key = jax.random.fold_in(key, 13)
    return window_lists(key, CBOXES, NCC, 3 * GCB)


def touch_ends(array, own_key, least, top_value):
    spot = [jax.random.randint(jax.random.fold_in(own_key, axis), (), 0, length) for axis, length in enumerate(array.shape)]
    main_axis = array.shape.index(max(array.shape))
    beside = spot[:main_axis] + [(spot[main_axis] + 1) % array.shape[main_axis]] + spot[main_axis + 1:]
    return array.at[tuple(spot)].set(least).at[tuple(beside)].set(top_value)


def level_of(key, shape, cuts, least, largest):
    level, own = 1.0, jax.random.fold_in(key, 6)
    for axis_at, parts in cuts:
        heights = jnp.exp(jax.random.uniform(jax.random.fold_in(own, axis_at), (parts,), jnp.float32, least / len(cuts), largest / len(cuts)))
        level = level * jnp.repeat(heights, shape[axis_at] // parts).reshape([-1 if axis == axis_at else 1 for axis in range(len(shape))])
    return level


def normal_values(stream_key, dims, scale, limit, shards=(), held_as=jnp.bfloat16):
    gain = level_of(stream_key, dims, shards, -0.22, 0.18) if shards else 1.0
    entries = jax.random.normal(stream_key, dims, jnp.float32) * scale * gain
    return jnp.minimum(jnp.maximum(entries, -limit), limit).astype(held_as)


def setup_inputs(seed: int = 0) -> dict:
    seeds = jax.random.split(jax.random.key(seed), 12)
    return {
        "dual_coeffs": normal_values(seeds[0], (S, BOXES), 1.0, 6.0, ((1, 512),)),
        "refine_select": touch_ends(jax.random.randint(seeds[1], (BOXES,), 0, RT), jax.random.fold_in(seeds[1], 1), 0, RT - 1).astype(jnp.int32),
        "refine_tiles": normal_values(seeds[2], (RT, SB, S), S ** -0.5, 1.0),
        "near_list": draw_near_list(jax.random.fold_in(seeds[11], 71), 0),
        "near_tiles": normal_values(seeds[4], (27, SB, SB), (SB * 4) ** -0.5, 0.25),
        "leaf_list": draw_leaf_list(jax.random.fold_in(seeds[11], 71), 0),
        "p2m": normal_values(seeds[6], (Q, SB), SB ** -0.5, 0.5),
        "m2m": normal_values(seeds[7], (8, Q, Q), (Q * 8) ** -0.5, 0.15625),
        "leaf_m2l": normal_values(seeds[8], (NC, Q, Q), (Q * NC) ** -0.5, 0.078125),
        "coarse_list": draw_coarse_list(jax.random.fold_in(seeds[11], 71), 0),
        "coarse_m2l": normal_values(seeds[10], (NCC, Q, Q), (Q * NCC) ** -0.5, 0.125),
    }


def select_apply(tiles, select, vectors, transpose):
    total = None
    for kind in range(tiles.shape[0]):
        tile = tiles[kind].astype(jnp.float32)
        if transpose:
            term = jnp.einsum("si,sb->ib", tile, vectors.astype(jnp.float32))
        else:
            term = jnp.einsum("is,sb->ib", tile, vectors.astype(jnp.float32))
        term = jnp.where(select[None, :] == kind, term, 0.0)
        total = term if total is None else total + term
    return total


def window_take(field, indices, offset, count):
    target = offset + indices
    valid = (indices >= 0) & (target >= 0) & (target < count)
    columns = jnp.take(field, jnp.clip(target, 0, count - 1).astype(jnp.int32), axis=1)
    return jnp.where(valid[None, :], columns, jnp.zeros_like(columns))


def class_sum(tables, field, lists, offset, count):
    total = jnp.zeros((tables.shape[1], lists.shape[0]), jnp.float32)
    for klass in range(lists.shape[1]):
        columns = window_take(field, lists[:, klass], offset, count)
        total = total + jnp.dot(tables[klass], columns, preferred_element_type=jnp.float32)
    return total


def reference(dual_coeffs, refine_select, refine_tiles, near_list, near_tiles, leaf_list, p2m, m2m, leaf_m2l, coarse_list, coarse_m2l):
    boxes = dual_coeffs.shape[1]
    coarse_count = boxes // 8
    refined = select_apply(refine_tiles, refine_select, dual_coeffs, False).astype(jnp.bfloat16)
    multipoles = jnp.dot(p2m, refined, preferred_element_type=jnp.float32).astype(jnp.bfloat16)
    positions = jnp.arange(boxes, dtype=jnp.int32)
    offset = (positions // BD) * BD - BD
    near_part = class_sum(near_tiles, refined, near_list, offset, boxes)
    leaf_local = class_sum(leaf_m2l, multipoles, leaf_list, offset, boxes)
    children = multipoles.astype(jnp.float32).reshape(Q, coarse_count, 8)
    coarse_mult = jnp.einsum("jqr,rpj->qp", m2m.astype(jnp.float32), children).astype(jnp.bfloat16)
    coarse_pos = jnp.arange(coarse_count, dtype=jnp.int32)
    coarse_offset = (coarse_pos // GCB) * GCB - GCB
    coarse_local = class_sum(coarse_m2l, coarse_mult, coarse_list, coarse_offset, coarse_count).astype(jnp.bfloat16)
    downward = jnp.einsum("jrq,rp->qpj", m2m.astype(jnp.float32), coarse_local.astype(jnp.float32)).reshape(Q, boxes)
    local_exp = (leaf_local + downward).astype(jnp.bfloat16)
    field = near_part + jnp.einsum("qs,qb->sb", p2m.astype(jnp.float32), local_exp.astype(jnp.float32))
    field = field.astype(jnp.bfloat16)
    return select_apply(refine_tiles, refine_select, field, True).astype(jnp.bfloat16)
```

```python
import functools

import jax
import jax.numpy as jnp
from jax import lax
from jax.experimental import pallas as pl
from jax.experimental.pallas import tpu as pltpu
from jax.sharding import PartitionSpec as P

F32 = jnp.float32
BF16 = jnp.bfloat16
NT = (((1,), (1,)), ((), ()))
TN = (((0,), (0,)), ((), ()))


def dot(a, b, dims=(((1,), (0,)), ((), ()))):
    return lax.dot_general(a, b, dims, preferred_element_type=F32)


def refine_rows(payload, joined):
    span = joined.shape[1] // 4
    values = payload[:span, :].astype(F32)
    kind = payload[span : span + 1, :].astype(F32)
    spread = jnp.concatenate([jnp.where(kind == k, values, 0.0) for k in range(4)], axis=0)
    return dot(jnp.transpose(spread).astype(BF16), joined, NT).astype(BF16)


def join_tiles(tiles_ref):
    return jnp.concatenate([tiles_ref[k] for k in range(4)], axis=1)


def upward_kernel(payload_ref, tiles_ref, p2m_ref, m2m_ref, out_ref, mult_ref):
    copies, coarse, _ = out_ref.shape
    order = p2m_ref.shape[0]
    refined = refine_rows(payload_ref[...], join_tiles(tiles_ref))
    mult = dot(refined, p2m_ref[...], NT).astype(BF16).astype(F32)
    mult_ref[0] = mult[:, :128]
    mult_ref[1, :, : order - 128] = mult[:, 128:]
    total = jnp.zeros((coarse, order), F32)
    for j in range(8):
        rows = [mult_ref[half, pl.ds(j, coarse, stride=8), :] for half in range(2)]
        rows = jnp.concatenate(rows, axis=1)[:, :order].astype(BF16)
        total = total + dot(rows, m2m_ref[j], NT)
    out_ref[...] = jnp.zeros_like(out_ref)
    for d in range(copies):
        out_ref[d, :, :order] = total.astype(BF16)


def near_leaf_kernel(
    own_ref, low_ref, high_ref, near_list_ref, leaf_list_ref, tiles_ref, near_ref, m2l_ref, p2m_ref,
    near_out, leaf_out, window, tail, lists, near_tab, leaf_tab, hot,
):
    boxes = own_ref.shape[1]
    order, width = p2m_ref.shape
    n_near, n_leaf = near_list_ref.shape[1], leaf_list_ref.shape[1]
    near_groups, leaf_groups = -(-n_near // 4), -(-n_leaf // 4)
    joined = join_tiles(tiles_ref)
    rows = jnp.concatenate(
        [refine_rows(ref[...], joined) for ref in (low_ref, own_ref, high_ref)], axis=0
    )
    for b in range(4):
        window[:, b * width : (b + 1) * width] = rows[b * 256 : (b + 1) * 256]
    tail[...] = jnp.zeros_like(tail)
    tail[:128, :width] = rows[1024:]
    tail[128:, width:] = rows[1024:]
    near_tab[...] = jnp.zeros_like(near_tab)
    for k in range(n_near):
        near_tab[k // 4, :, (k % 4) * width : (k % 4 + 1) * width] = near_ref[k]
    for c in range(n_leaf):
        leaf_tab[c // 4, :order, (c % 4) * width : (c % 4 + 1) * width] = dot(
            m2l_ref[c], p2m_ref[...]
        ).astype(BF16)
    lists[...] = jnp.full_like(lists, -1)
    lists[0, :, :n_near] = near_list_ref[...]
    lists[1, :, :n_leaf] = leaf_list_ref[...]
    near_out[...] = jnp.zeros_like(near_out)
    leaf_out[...] = jnp.zeros_like(leaf_out)
    spot = lax.broadcasted_iota(jnp.int32, (boxes, 256), 1)

    def group(which, g, table, out):
        columns = pltpu.roll(lists[which], lax.rem(128 - 4 * g, 128), 1)
        index = [columns[:, c : c + 1] for c in range(4)]
        for c in range(4):
            hot[c * boxes : (c + 1) * boxes, :] = jnp.where(
                (index[c] & 255) == spot, 1.0, 0.0
            ).astype(BF16)
        first = dot(hot[...], window[:, : 2 * width])
        second = dot(hot[...], window[:, 2 * width :])
        picked = []
        for c in range(4):
            if c % 2 == 0:
                pair = jnp.concatenate(
                    [hot[c * boxes : (c + 1) * boxes, :128], hot[(c + 1) * boxes : (c + 2) * boxes, :128]],
                    axis=1,
                )
                last = dot(pair, tail[...])
            at = slice(c * boxes, (c + 1) * boxes)
            block = jnp.broadcast_to(index[c] >> 8, (boxes, width))
            value = jnp.where(block == 4, last[:, (c % 2) * width : (c % 2 + 1) * width], 0.0)
            value = jnp.where(block == 3, second[at, width:], value)
            value = jnp.where(block == 2, second[at, :width], value)
            value = jnp.where(block == 1, first[at, width:], value)
            value = jnp.where(block == 0, first[at, :width], value)
            picked.append(value.astype(BF16))
        out[...] += dot(jnp.concatenate(picked, axis=1), table[g], NT)

    def near_step(g, carry):
        group(0, g, near_tab, near_out)
        return carry

    def leaf_step(g, carry):
        group(1, g, leaf_tab, leaf_out)
        return carry

    lax.fori_loop(0, near_groups, near_step, 0)
    lax.fori_loop(0, leaf_groups, leaf_step, 0)


def downward_kernel(
    near_part_ref, leaf_local_ref, slab_ref, low_ref, high_ref, list_ref, payload_ref,
    tiles_ref, p2m_ref, m2m_ref, m2l_ref, out_ref, down,
):
    order = p2m_ref.shape[0]
    coarse, classes = list_ref.shape
    span = out_ref.shape[0]
    index = list_ref[...]
    window = jnp.concatenate([low_ref[...], slab_ref[...], high_ref[...]], axis=0)
    spot = lax.broadcasted_iota(jnp.int32, (coarse, window.shape[0]), 1)
    hot = jnp.concatenate(
        [jnp.where(index[:, c : c + 1] == spot, 1.0, 0.0).astype(BF16) for c in range(classes)], axis=0
    )
    picked = dot(hot, window).astype(BF16)
    total = jnp.zeros((coarse, order), F32)
    for c in range(classes):
        total = total + dot(picked[c * coarse : (c + 1) * coarse, :order], m2l_ref[c], NT)
    local = total.astype(BF16)
    for j in range(8):
        part = dot(local, m2m_ref[j])
        down[0, pl.ds(j, coarse, stride=8), :] = part[:, :128]
        down[1, pl.ds(j, coarse, stride=8), : order - 128] = part[:, 128:]
    expansion = jnp.concatenate([down[0], down[1]], axis=1)[:, :order]
    expansion = (leaf_local_ref[:, :order] + expansion).astype(BF16)
    field = (near_part_ref[...] + dot(expansion, p2m_ref[...])).astype(BF16)
    by_kind = dot(join_tiles(tiles_ref), field, (((0,), (1,)), ((), ())))
    kind = payload_ref[span : span + 1, :].astype(F32)
    tested = jnp.zeros(out_ref.shape, F32)
    for k in range(4):
        tested = jnp.where(kind == k, by_kind[k * span : (k + 1) * span], tested)
    out_ref[...] = tested.astype(BF16)


def call(kernel, outs, scratch, args, flops, megabytes):
    return pl.pallas_call(
        kernel,
        out_shape=outs,
        in_specs=[pl.BlockSpec(memory_space=pltpu.VMEM)] * len(args),
        out_specs=jax.tree.map(lambda _: pl.BlockSpec(memory_space=pltpu.VMEM), outs),
        scratch_shapes=scratch,
        compiler_params=pltpu.CompilerParams(vmem_limit_bytes=40 * 1024 * 1024),
        cost_estimate=pl.CostEstimate(
            flops=flops, bytes_accessed=int(megabytes * 1e6), transcendentals=0
        ),
    )(*args)


def shifted(block, axis, step):
    count = lax.axis_size(axis)
    return lax.ppermute(block, axis, [(i, i + step) for i in range(count) if 0 <= i + step < count])


def body(
    dual_coeffs, refine_select, refine_tiles, near_list, near_tiles, leaf_list, p2m, m2m, leaf_m2l,
    coarse_list, coarse_m2l,
):
    span, boxes = dual_coeffs.shape
    order, width = p2m.shape
    coarse = boxes // 8
    subs = lax.axis_size("sub")
    kinds = jnp.broadcast_to(refine_select[None, :], (8, boxes)).astype(BF16)
    payload = jnp.concatenate([dual_coeffs, kinds], axis=0)
    low = shifted(payload, ("grp", "sub"), 1)
    high = shifted(payload, ("grp", "sub"), -1)
    mine = call(
        upward_kernel,
        jax.ShapeDtypeStruct((subs, coarse, 256), BF16),
        [pltpu.VMEM((2, boxes, 128), F32)],
        (payload, refine_tiles, p2m, m2m),
        100_000_000, 1.0,
    )
    slab = lax.all_to_all(mine, "sub", 0, 0).reshape(subs * coarse, 256)
    near_part, leaf_local = call(
        near_leaf_kernel,
        (jax.ShapeDtypeStruct((boxes, width), F32), jax.ShapeDtypeStruct((boxes, 176), F32)),
        [
            pltpu.VMEM((256, 4 * width), BF16),
            pltpu.VMEM((256, 2 * width), BF16),
            pltpu.VMEM((2, boxes, 128), jnp.int32),
            pltpu.VMEM((7, width, 4 * width), BF16),
            pltpu.VMEM((8, 176, 4 * width), BF16),
            pltpu.VMEM((4 * boxes, 256), BF16),
        ],
        (payload, low, high, near_list, leaf_list, refine_tiles, near_tiles, leaf_m2l, p2m),
        10_000_000_000, 5.0,
    )
    slab_low = shifted(slab, "grp", 1)
    slab_high = shifted(slab, "grp", -1)
    return call(
        downward_kernel,
        jax.ShapeDtypeStruct((span, boxes), BF16),
        [pltpu.VMEM((2, boxes, 128), F32)],
        (
            near_part, leaf_local, slab, slab_low, slab_high, coarse_list, payload, refine_tiles, p2m,
            m2m, coarse_m2l,
        ),
        1_000_000_000, 3.0,
    )


def solution(mesh):
    placed = (
        P(None, ("grp", "sub")),
        P(("grp", "sub")),
        P(),
        P(("grp", "sub"), None),
        P(),
        P(("grp", "sub"), None),
        P(),
        P(),
        P(),
        P(("grp", "sub"), None),
        P(),
    )
    return jax.shard_map(
        body, mesh=mesh, in_specs=placed, out_specs=P(None, ("grp", "sub")), check_vma=False
    )
```

```python
import functools

import jax
import jax.numpy as jnp
from jax import lax
from jax.experimental import pallas as pl
from jax.experimental.pallas import tpu as pltpu
from jax.sharding import PartitionSpec as P

F32 = jnp.float32
BF16 = jnp.bfloat16
NT = (((1,), (1,)), ((), ()))
TN = (((0,), (0,)), ((), ()))


def dot(a, b, dims=(((1,), (0,)), ((), ()))):
    return lax.dot_general(a, b, dims, preferred_element_type=F32)


def refine_rows(payload, joined):
    span = joined.shape[0] // 4
    values = payload[:span, :].astype(F32)
    kind = payload[span : span + 1, :].astype(F32)
    spread = jnp.concatenate([jnp.where(kind == k, values, 0.0) for k in range(4)], axis=0)
    return dot(jnp.transpose(spread).astype(BF16), joined).astype(BF16)


def upward_kernel(
    dual_ref, select_ref, joined_ref, p2m_ref, m2m_ref, payload_ref, out_ref, table_ref, product, refined
):
    copies, coarse, _ = out_ref.shape
    order, width = p2m_ref.shape
    span = dual_ref.shape[0]
    payload_ref[:span] = dual_ref[...]
    payload_ref[span:] = jnp.broadcast_to(select_ref[...], (8, select_ref.shape[1])).astype(F32).astype(BF16)
    product[...] = dot(m2m_ref[...], p2m_ref[...])
    refined[...] = refine_rows(payload_ref[...], joined_ref[...]).astype(F32)
    total = jnp.zeros((coarse, order), F32)
    for j in range(0, 8, 2):
        tables, rows = [], []
        for i in (j, j + 1):
            table = product[pl.ds(i, order, stride=8), :].astype(BF16)
            table_ref[i, :order] = table
            tables.append(table)
            rows.append(refined[pl.ds(i, coarse, stride=8), :].astype(BF16))
        total = total + dot(jnp.concatenate(rows, axis=1), jnp.concatenate(tables, axis=1), NT)
    out_ref[...] = jnp.zeros_like(out_ref)
    for d in range(copies):
        out_ref[d, :, :order] = total.astype(BF16)


def near_leaf_kernel(
    own_ref, low_ref, high_ref, near_list_ref, leaf_list_ref, joined_ref, near_ref, m2l_ref, p2m_ref,
    near_out, leaf_out, window, tail, lists, near_tab, leaf_tab, hot, product,
):
    boxes = own_ref.shape[1]
    order, width = p2m_ref.shape
    n_near, n_leaf = near_list_ref.shape[0], leaf_list_ref.shape[0]
    near_groups, leaf_groups = -(-n_near // 4), -(-n_leaf // 4)
    rows = jnp.concatenate(
        [refine_rows(ref[...], joined_ref[...]) for ref in (low_ref, own_ref, high_ref)], axis=0
    )
    for b in range(4):
        window[:, b * width : (b + 1) * width] = rows[b * 256 : (b + 1) * 256]
    tail[...] = jnp.zeros_like(tail)
    tail[:128, :width] = rows[1024:]
    tail[128:, width:] = rows[1024:]
    near_tab[...] = jnp.zeros_like(near_tab)
    for k in range(n_near):
        near_tab[k // 4, :, (k % 4) * width : (k % 4 + 1) * width] = near_ref[k]
    product[...] = dot(m2l_ref[...], p2m_ref[...])
    for c in range(n_leaf):
        leaf_tab[c // 4, :order, (c % 4) * width : (c % 4 + 1) * width] = product[
            pl.ds(c, order, stride=n_leaf), :
        ].astype(BF16)
    for at, ref in ((0, near_list_ref), (1, leaf_list_ref)):
        padded = jnp.concatenate(
            [ref[...], jnp.full((128 - ref.shape[0], boxes), -1, jnp.int32)], axis=0
        )
        lists[at] = jnp.transpose(padded)
    near_out[...] = jnp.zeros_like(near_out)
    leaf_out[...] = jnp.zeros_like(leaf_out)
    spot = lax.broadcasted_iota(jnp.int32, (boxes, 256), 1)

    def group(which, g, table, out):
        columns = pltpu.roll(lists[which], lax.rem(128 - 4 * g, 128), 1)
        index = [columns[:, c : c + 1] for c in range(4)]
        for c in range(4):
            hot[c * boxes : (c + 1) * boxes, :] = jnp.where(
                (index[c] & 255) == spot, 1.0, 0.0
            ).astype(BF16)
        first = dot(hot[...], window[:, : 2 * width])
        second = dot(hot[...], window[:, 2 * width :])
        picked = []
        for c in range(4):
            if c % 2 == 0:
                pair = jnp.concatenate(
                    [hot[c * boxes : (c + 1) * boxes, :128], hot[(c + 1) * boxes : (c + 2) * boxes, :128]],
                    axis=1,
                )
                last = dot(pair, tail[...])
            at = slice(c * boxes, (c + 1) * boxes)
            block = jnp.broadcast_to(index[c] >> 8, (boxes, width))
            value = jnp.where(block == 4, last[:, (c % 2) * width : (c % 2 + 1) * width], 0.0)
            value = jnp.where(block == 3, second[at, width:], value)
            value = jnp.where(block == 2, second[at, :width], value)
            value = jnp.where(block == 1, first[at, width:], value)
            value = jnp.where(block == 0, first[at, :width], value)
            picked.append(value.astype(BF16))
        out[...] += dot(jnp.concatenate(picked, axis=1), table[g], NT)

    def near_step(g, carry):
        group(0, g, near_tab, near_out)
        return carry

    def leaf_step(g, carry):
        group(1, g, leaf_tab, leaf_out)
        return carry

    lax.fori_loop(0, near_groups, near_step, 0)
    lax.fori_loop(0, leaf_groups, leaf_step, 0)


def table_kernel(m2l_ref, out_ref, wide):
    classes, order, _ = out_ref.shape
    wide[0] = m2l_ref[:, :128].astype(F32)
    wide[1, :, : order - 128] = m2l_ref[:, 128:].astype(F32)
    for c in range(classes):
        rows = [wide[half, pl.ds(c, order, stride=classes), :] for half in range(2)]
        out_ref[c] = jnp.concatenate(rows, axis=1)[:, :order].astype(BF16)


def downward_kernel(
    near_part_ref, leaf_local_ref, slab_ref, low_ref, high_ref, list_ref, payload_ref,
    joined_ref, p2m_ref, table_ref, m2l_ref, out_ref, down,
):
    order = p2m_ref.shape[0]
    classes, coarse = list_ref.shape
    span = out_ref.shape[0]
    index = jnp.transpose(list_ref[...])
    window = jnp.concatenate([low_ref[...], slab_ref[...], high_ref[...]], axis=0)
    spot = lax.broadcasted_iota(jnp.int32, (coarse, window.shape[0]), 1)
    hot = jnp.concatenate(
        [jnp.where(index[:, c : c + 1] == spot, 1.0, 0.0).astype(BF16) for c in range(classes)], axis=0
    )
    picked = dot(hot, window).astype(BF16)
    total = jnp.zeros((coarse, order), F32)
    for c in range(classes):
        total = total + dot(picked[c * coarse : (c + 1) * coarse, :order], m2l_ref[c], NT)
    local = total.astype(BF16)
    for j in range(8):
        down[pl.ds(j, coarse, stride=8), :] = dot(local, table_ref[j, :order])
    leaf = leaf_local_ref[:, :order].astype(BF16)
    field = (near_part_ref[...] + dot(leaf, p2m_ref[...]) + down[...]).astype(BF16)
    by_kind = dot(joined_ref[...], field, NT)
    kind = payload_ref[span : span + 1, :].astype(F32)
    tested = jnp.zeros(out_ref.shape, F32)
    for k in range(4):
        tested = jnp.where(kind == k, by_kind[k * span : (k + 1) * span], tested)
    out_ref[...] = tested.astype(BF16)


def call(kernel, outs, scratch, args, flops, megabytes):
    return pl.pallas_call(
        kernel,
        out_shape=outs,
        in_specs=[pl.BlockSpec(memory_space=pltpu.VMEM)] * len(args),
        out_specs=jax.tree.map(lambda _: pl.BlockSpec(memory_space=pltpu.VMEM), outs),
        scratch_shapes=scratch,
        compiler_params=pltpu.CompilerParams(vmem_limit_bytes=40 * 1024 * 1024),
        cost_estimate=pl.CostEstimate(
            flops=flops, bytes_accessed=int(megabytes * 1e6), transcendentals=0
        ),
    )(*args)


def shifted(block, axis, step):
    count = lax.axis_size(axis)
    return lax.ppermute(block, axis, [(i, i + step) for i in range(count) if 0 <= i + step < count])


def body(
    dual_coeffs, refine_select, refine_tiles, near_list, near_tiles, leaf_list, p2m, m2m, leaf_m2l,
    coarse_list, coarse_m2l,
):
    span, boxes = dual_coeffs.shape
    order, width = p2m.shape
    coarse = boxes // 8
    subs = lax.axis_size("sub")
    joined = jnp.transpose(refine_tiles, (0, 2, 1)).reshape(4 * span, width)
    m2m_rows = jnp.transpose(m2m, (1, 0, 2)).reshape(-1, order)
    leaf_rows = jnp.transpose(leaf_m2l, (1, 0, 2)).reshape(-1, order)
    coarse_rows = jnp.transpose(coarse_m2l, (1, 0, 2)).reshape(-1, order)
    payload, mine, table = call(
        upward_kernel,
        (
            jax.ShapeDtypeStruct((span + 8, boxes), BF16),
            jax.ShapeDtypeStruct((subs, coarse, 256), BF16),
            jax.ShapeDtypeStruct((8, 176, width), BF16),
        ),
        [pltpu.VMEM((8 * order, width), F32), pltpu.VMEM((boxes, width), F32)],
        (dual_coeffs, refine_select.reshape(1, boxes), joined, p2m, m2m_rows),
        100_000_000, 1.0,
    )
    low = shifted(payload, ("grp", "sub"), 1)
    high = shifted(payload, ("grp", "sub"), -1)
    slab = lax.all_to_all(mine, "sub", 0, 0).reshape(subs * coarse, 256)
    near_part, leaf_local = call(
        near_leaf_kernel,
        (jax.ShapeDtypeStruct((boxes, width), F32), jax.ShapeDtypeStruct((boxes, 176), F32)),
        [
            pltpu.VMEM((256, 4 * width), BF16),
            pltpu.VMEM((256, 2 * width), BF16),
            pltpu.VMEM((2, boxes, 128), jnp.int32),
            pltpu.VMEM((7, width, 4 * width), BF16),
            pltpu.VMEM((8, 176, 4 * width), BF16),
            pltpu.VMEM((4 * boxes, 256), BF16),
            pltpu.VMEM((32 * order, width), F32),
        ],
        (payload, low, high, near_list.T, leaf_list.T, joined, near_tiles, leaf_rows, p2m),
        10_000_000_000, 5.0,
    )
    slab_low = shifted(slab, "grp", 1)
    slab_high = shifted(slab, "grp", -1)
    coarse_table = call(
        table_kernel,
        jax.ShapeDtypeStruct(coarse_m2l.shape, BF16),
        [pltpu.VMEM((2, 16 * order, 128), F32)],
        (coarse_rows,),
        100_000_000, 3.0,
    )
    return call(
        downward_kernel,
        jax.ShapeDtypeStruct((span, boxes), BF16),
        [pltpu.VMEM((boxes, width), F32)],
        (
            near_part, leaf_local, slab, slab_low, slab_high, coarse_list.T, payload, joined, p2m,
            table, coarse_table,
        ),
        1_000_000_000, 3.0,
    )


def solution(mesh):
    placed = (
        P(None, ("grp", "sub")),
        P(("grp", "sub")),
        P(),
        P(("grp", "sub"), None),
        P(),
        P(("grp", "sub"), None),
        P(),
        P(),
        P(),
        P(("grp", "sub"), None),
        P(),
    )
    return jax.shard_map(
        body, mesh=mesh, in_specs=placed, out_specs=P(None, ("grp", "sub")), check_vma=False
    )
```

```python
import jax
import jax.numpy as jnp
from jax import lax
from jax.experimental import pallas as pl
from jax.experimental.pallas import tpu as pltpu
from jax.sharding import PartitionSpec as P

GROUP = 8
F32 = jnp.float32
BF16 = jnp.bfloat16
NT = (((1,), (1,)), ((), ()))
TN = (((0,), (0,)), ((), ()))


def dot(a, b, dims=(((1,), (0,)), ((), ()))):
    return lax.dot_general(a, b, dims, preferred_element_type=F32)


def refine_rows(payload, joined):
    span = joined.shape[0] // 4
    values = payload[:span, :].astype(F32)
    kind = payload[span : span + 1, :].astype(F32)
    spread = jnp.concatenate([jnp.where(kind == k, values, 0.0) for k in range(4)], axis=0)
    return dot(jnp.transpose(spread).astype(BF16), joined).astype(BF16)


def fetch(sources, targets, sems):
    copies = [
        pltpu.make_async_copy(source, target, sems.at[i])
        for i, (source, target) in enumerate(zip(sources, targets))
    ]
    for copy in copies:
        copy.start()
    return copies


def upward_kernel(
    dual_hbm, select_ref, joined_hbm, p2m_hbm, m2m_hbm, payload_ref, out_ref, table_ref,
    dual, joined, p2m, m2m, product, refined, sems,
):
    copies = fetch((dual_hbm, joined_hbm, p2m_hbm, m2m_hbm), (dual, joined, p2m, m2m), sems)
    subs, coarse, _ = out_ref.shape
    order, width = p2m.shape
    span, boxes = dual.shape
    payload_ref[span:] = jnp.broadcast_to(select_ref[...], (8, boxes)).astype(F32).astype(BF16)
    out_ref[...] = jnp.zeros_like(out_ref)
    for copy in copies:
        copy.wait()
    payload_ref[:span] = dual[...]
    product[...] = dot(m2m[...], p2m[...])
    refined[...] = refine_rows(payload_ref[...], joined[...]).astype(F32)
    total = jnp.zeros((coarse, order), F32)
    for j in range(0, 8, 2):
        tables, rows = [], []
        for i in (j, j + 1):
            table = product[pl.ds(i, order, stride=8), :].astype(BF16)
            table_ref[i, :order] = table
            tables.append(table)
            rows.append(refined[pl.ds(i, coarse, stride=8), :].astype(BF16))
        total = total + dot(jnp.concatenate(rows, axis=1), jnp.concatenate(tables, axis=1), NT)
    for d in range(subs):
        out_ref[d, :, :order] = total.astype(BF16)


def near_leaf_kernel(
    own_ref, low_ref, high_ref, near_list_ref, leaf_list_ref, joined_ref, near_ref, m2l_hbm, p2m_ref,
    field_ref, window, near_index, leaf_index, near_tab, leaf_tab, m2l, product, leaf_local, sems,
):
    copies = fetch((m2l_hbm,), (m2l,), sems)
    depth, boxes = own_ref.shape
    order, width = p2m_ref.shape
    span = depth - 8
    n_near, n_leaf = near_list_ref.shape[0], leaf_list_ref.shape[0]
    whole = jnp.concatenate(
        [low_ref[...], own_ref[...], high_ref[...], jnp.zeros((depth, 128), BF16)], axis=1
    ).astype(F32)
    blocks = whole.shape[1] // 256
    window[...] = jnp.concatenate(
        [whole[:, b * 256 : (b + 1) * 256] for b in range(blocks)], axis=0
    ).astype(BF16)
    spot = lax.broadcasted_iota(jnp.int32, (256, boxes), 0).astype(BF16)

    def hot_of(index):
        low = (index & 255).astype(F32).astype(BF16)
        return jnp.where(low == spot, jnp.array(1.0, BF16), jnp.array(0.0, BF16))

    def expand(index, got):
        block = index >> 8
        value = jnp.zeros((depth, boxes), F32)
        for b in range(blocks):
            value = jnp.where(block == b, got[b * depth : (b + 1) * depth], value)
        kind = value[span : span + 1]
        return [jnp.where(kind == k, value[:span], 0.0) for k in range(4)]

    def group(rows, table, out):
        index = [rows[c : c + 1, :] for c in range(GROUP)]
        got = dot(window[...], jnp.concatenate([hot_of(i) for i in index], axis=1))
        parts = []
        for c in range(GROUP):
            parts += expand(index[c], got[:, c * boxes : (c + 1) * boxes])
        out[...] += dot(table, jnp.concatenate(parts, axis=0).astype(BF16))

    joined = joined_ref[...]
    near_tab[...] = jnp.zeros_like(near_tab)
    near_index[...] = jnp.full_like(near_index, -1)
    for k in range(n_near):
        at = slice((k % GROUP) * width, (k % GROUP + 1) * width)
        near_tab[k // GROUP, :, at] = dot(near_ref[k], joined, NT).astype(BF16)
        near_index[k // GROUP, k % GROUP : k % GROUP + 1] = near_list_ref[k : k + 1]
    field_ref[...] = jnp.zeros_like(field_ref)
    for g in range(near_index.shape[0]):
        group(near_index[g], near_tab[g], field_ref)

    spread = dot(p2m_ref[...], joined, NT).astype(BF16)
    for copy in copies:
        copy.wait()
    product[...] = dot(m2l[...], spread)
    for c in range(n_leaf):
        at = slice((c % GROUP) * width, (c % GROUP + 1) * width)
        leaf_tab[c // GROUP, :order, at] = product[pl.ds(c, order, stride=n_leaf), :].astype(BF16)
        leaf_index[c // GROUP, c % GROUP : c % GROUP + 1] = leaf_list_ref[c : c + 1]
    leaf_local[...] = jnp.zeros_like(leaf_local)
    for g in range(leaf_index.shape[0]):
        group(leaf_index[g], leaf_tab[g], leaf_local)
    field_ref[...] += dot(p2m_ref[...], leaf_local[:order].astype(BF16), TN)


def table_kernel(m2l_ref, out_ref, wide):
    classes, order, _ = out_ref.shape
    wide[0] = m2l_ref[:, :128].astype(F32)
    wide[1, :, : order - 128] = m2l_ref[:, 128:].astype(F32)
    for c in range(classes):
        rows = [wide[half, pl.ds(c, order, stride=classes), :] for half in range(2)]
        out_ref[c] = jnp.concatenate(rows, axis=1)[:, :order].astype(BF16)


def downward_kernel(
    field_ref, slab_ref, low_ref, high_ref, list_ref, payload_ref, joined_ref, table_ref, m2l_ref,
    out_ref, down,
):
    order = m2l_ref.shape[1]
    classes, coarse = list_ref.shape
    span = out_ref.shape[0]
    index = jnp.transpose(list_ref[...])
    window = jnp.concatenate([low_ref[...], slab_ref[...], high_ref[...]], axis=0)
    spot = lax.broadcasted_iota(jnp.int32, (coarse, window.shape[0]), 1)
    hot = jnp.concatenate(
        [jnp.where(index[:, c : c + 1] == spot, 1.0, 0.0).astype(BF16) for c in range(classes)], axis=0
    )
    picked = dot(hot, window).astype(BF16)
    total = jnp.zeros((coarse, order), F32)
    for c in range(classes):
        total = total + dot(picked[c * coarse : (c + 1) * coarse, :order], m2l_ref[c], NT)
    local = total.astype(BF16)
    for j in range(8):
        down[pl.ds(j, coarse, stride=8), :] = dot(local, table_ref[j, :order])
    field = (field_ref[...] + jnp.transpose(down[...])).astype(BF16)
    by_kind = dot(joined_ref[...], field)
    kind = payload_ref[span : span + 1, :].astype(F32)
    tested = jnp.zeros(out_ref.shape, F32)
    for k in range(4):
        tested = jnp.where(kind == k, by_kind[k * span : (k + 1) * span], tested)
    out_ref[...] = tested.astype(BF16)


def call(kernel, outs, scratch, args, flops, megabytes, in_hbm=()):
    return pl.pallas_call(
        kernel,
        out_shape=outs,
        in_specs=[
            pl.BlockSpec(memory_space=pltpu.HBM if i in in_hbm else pltpu.VMEM)
            for i in range(len(args))
        ],
        out_specs=jax.tree.map(lambda _: pl.BlockSpec(memory_space=pltpu.VMEM), outs),
        scratch_shapes=scratch,
        compiler_params=pltpu.CompilerParams(vmem_limit_bytes=40 * 1024 * 1024),
        cost_estimate=pl.CostEstimate(
            flops=flops, bytes_accessed=int(megabytes * 1e6), transcendentals=0
        ),
    )(*args)


def shifted(block, axis, step):
    count = lax.axis_size(axis)
    return lax.ppermute(block, axis, [(i, i + step) for i in range(count) if 0 <= i + step < count])


def body(
    dual_coeffs, refine_select, refine_tiles, near_list, near_tiles, leaf_list, p2m, m2m, leaf_m2l,
    coarse_list, coarse_m2l,
):
    span, boxes = dual_coeffs.shape
    order, width = p2m.shape
    coarse = boxes // 8
    subs = lax.axis_size("sub")
    joined = jnp.transpose(refine_tiles, (0, 2, 1)).reshape(4 * span, width)
    m2m_rows = jnp.transpose(m2m, (1, 0, 2)).reshape(-1, order)
    leaf_rows = jnp.transpose(leaf_m2l, (1, 0, 2)).reshape(-1, order)
    coarse_rows = jnp.transpose(coarse_m2l, (1, 0, 2)).reshape(-1, order)
    payload, mine, table = call(
        upward_kernel,
        (
            jax.ShapeDtypeStruct((span + 8, boxes), BF16),
            jax.ShapeDtypeStruct((subs, coarse, 256), BF16),
            jax.ShapeDtypeStruct((8, 176, width), BF16),
        ),
        [pltpu.VMEM(a.shape, BF16) for a in (dual_coeffs, joined, p2m, m2m_rows)]
        + [
            pltpu.VMEM((8 * order, width), F32),
            pltpu.VMEM((boxes, width), F32),
            pltpu.SemaphoreType.DMA((4,)),
        ],
        (dual_coeffs, refine_select.reshape(1, boxes), joined, p2m, m2m_rows),
        100_000_000, 1.0, (0, 2, 3, 4),
    )
    low = shifted(payload, ("grp", "sub"), 1)
    high = shifted(payload, ("grp", "sub"), -1)
    slab = lax.all_to_all(mine, "sub", 0, 0).reshape(subs * coarse, 256)
    near_groups, leaf_groups = -(-near_tiles.shape[0] // GROUP), leaf_m2l.shape[0] // GROUP
    field = call(
        near_leaf_kernel,
        jax.ShapeDtypeStruct((width, boxes), F32),
        [
            pltpu.VMEM((5 * (span + 8), 256), BF16),
            pltpu.VMEM((near_groups, GROUP, boxes), jnp.int32),
            pltpu.VMEM((leaf_groups, GROUP, boxes), jnp.int32),
            pltpu.VMEM((near_groups, width, GROUP * width), BF16),
            pltpu.VMEM((leaf_groups, 176, GROUP * width), BF16),
            pltpu.VMEM(leaf_rows.shape, BF16),
            pltpu.VMEM((leaf_rows.shape[0], width), F32),
            pltpu.VMEM((176, boxes), F32),
            pltpu.SemaphoreType.DMA((1,)),
        ],
        (payload, low, high, near_list.T, leaf_list.T, joined, near_tiles, leaf_rows, p2m),
        5_000_000_000, 5.0, (7,),
    )
    slab_low = shifted(slab, "grp", 1)
    slab_high = shifted(slab, "grp", -1)
    coarse_table = call(
        table_kernel,
        jax.ShapeDtypeStruct(coarse_m2l.shape, BF16),
        [pltpu.VMEM((2, 16 * order, 128), F32)],
        (coarse_rows,),
        100_000_000, 3.0,
    )
    return call(
        downward_kernel,
        jax.ShapeDtypeStruct((span, boxes), BF16),
        [pltpu.VMEM((boxes, width), F32)],
        (
            field, slab, slab_low, slab_high, coarse_list.T, payload, joined, table, coarse_table,
        ),
        1_000_000_000, 3.0,
    )


def solution(mesh):
    placed = (
        P(None, ("grp", "sub")),
        P(("grp", "sub")),
        P(),
        P(("grp", "sub"), None),
        P(),
        P(("grp", "sub"), None),
        P(),
        P(),
        P(),
        P(("grp", "sub"), None),
        P(),
    )
    return jax.shard_map(
        body, mesh=mesh, in_specs=placed, out_specs=P(None, ("grp", "sub")), check_vma=False
    )
```

```python
import jax
import jax.numpy as jnp
from jax import lax
from jax.experimental import pallas as pl
from jax.experimental.pallas import tpu as pltpu
from jax.sharding import PartitionSpec as P

GROUP = 8
F32 = jnp.float32
BF16 = jnp.bfloat16
NT = (((1,), (1,)), ((), ()))
TN = (((0,), (0,)), ((), ()))


def dot(a, b, dims=(((1,), (0,)), ((), ()))):
    return lax.dot_general(a, b, dims, preferred_element_type=F32)


def refine_rows(payload, joined):
    span = joined.shape[0] // 4
    values = payload[:span, :].astype(F32)
    kind = payload[span : span + 1, :].astype(F32)
    spread = jnp.concatenate([jnp.where(kind == k, values, 0.0) for k in range(4)], axis=0)
    return dot(jnp.transpose(spread).astype(BF16), joined).astype(BF16)


def fetch(sources, targets, sems):
    copies = [
        pltpu.make_async_copy(source, target, sems.at[i])
        for i, (source, target) in enumerate(zip(sources, targets))
    ]
    for copy in copies:
        copy.start()
    return copies


def upward_kernel(
    dual_hbm, select_hbm, joined_hbm, p2m_hbm, m2m_hbm, payload_ref, out_ref, table_ref,
    dual, select, joined, p2m, m2m, product, refined, sems,
):
    copies = fetch(
        (dual_hbm, select_hbm, joined_hbm, p2m_hbm, m2m_hbm), (dual, select, joined, p2m, m2m), sems
    )
    subs, coarse, _ = out_ref.shape
    order, width = p2m.shape
    span, boxes = dual.shape
    out_ref[...] = jnp.zeros_like(out_ref)
    for copy in copies:
        copy.wait()
    payload_ref[:span] = dual[...]
    kind = select[...].reshape(1, boxes)
    payload_ref[span:] = jnp.broadcast_to(kind, (8, boxes)).astype(F32).astype(BF16)
    product[...] = dot(m2m[...], p2m[...])
    refined[...] = refine_rows(payload_ref[...], joined[...]).astype(F32)
    total = jnp.zeros((coarse, order), F32)
    for j in range(0, 8, 2):
        tables, rows = [], []
        for i in (j, j + 1):
            table = product[pl.ds(i, order, stride=8), :].astype(BF16)
            table_ref[i, :order] = table
            tables.append(table)
            rows.append(refined[pl.ds(i, coarse, stride=8), :].astype(BF16))
        total = total + dot(jnp.concatenate(rows, axis=1), jnp.concatenate(tables, axis=1), NT)
    for d in range(subs):
        out_ref[d, :, :order] = total.astype(BF16)


class Picker:
    def __init__(self, own_ref, low_ref, high_ref, window):
        self.depth, self.boxes = own_ref.shape
        self.window = window
        whole = jnp.concatenate(
            [low_ref[...], own_ref[...], high_ref[...], jnp.zeros((self.depth, 128), BF16)], axis=1
        ).astype(F32)
        self.blocks = whole.shape[1] // 256
        window[...] = jnp.concatenate(
            [whole[:, b * 256 : (b + 1) * 256] for b in range(self.blocks)], axis=0
        ).astype(BF16)
        self.spot = lax.broadcasted_iota(jnp.int32, (256, self.boxes), 0).astype(BF16)

    def hot(self, index):
        low = (index & 255).astype(F32).astype(BF16)
        return jnp.where(low == self.spot, jnp.array(1.0, BF16), jnp.array(0.0, BF16))

    def expand(self, index, got):
        block, depth = index >> 8, self.depth
        value = jnp.zeros((depth, self.boxes), F32)
        for b in range(self.blocks):
            value = jnp.where(block == b, got[b * depth : (b + 1) * depth], value)
        kind = value[depth - 8 : depth - 7]
        return [jnp.where(kind == k, value[: depth - 8], 0.0) for k in range(4)]

    def add(self, index, table, out):
        boxes = self.boxes
        got = dot(self.window[...], jnp.concatenate([self.hot(i) for i in index], axis=1))
        parts = []
        for c, i in enumerate(index):
            parts += self.expand(i, got[:, c * boxes : (c + 1) * boxes])
        out[...] += dot(table, jnp.concatenate(parts, axis=0).astype(BF16))


def leaf_kernel(
    own_ref, low_ref, high_ref, list_hbm, joined_hbm, p2m_hbm, m2l_hbm, coarse_hbm, field_ref, coarse_ref,
    list_ref, joined_ref, p2m_ref, m2l, coarse, window, table, product, wide, local, sems,
):
    copies = fetch(
        (list_hbm, joined_hbm, p2m_hbm, m2l_hbm, coarse_hbm),
        (list_ref, joined_ref, p2m_ref, m2l, coarse),
        sems,
    )
    picker = Picker(own_ref, low_ref, high_ref, window)
    for copy in copies[:3]:
        copy.wait()
    order, width = p2m_ref.shape
    classes = list_ref.shape[0]
    spread = dot(p2m_ref[...], joined_ref[...], NT).astype(BF16)
    local[...] = jnp.zeros_like(local)
    copies[3].wait()
    product[...] = dot(m2l[...], spread)
    for c in range(classes):
        at = slice((c % GROUP) * width, (c % GROUP + 1) * width)
        table[c // GROUP, :order, at] = product[pl.ds(c, order, stride=classes), :].astype(BF16)
    for g in range(classes // GROUP):
        index = [list_ref[c : c + 1, :] for c in range(g * GROUP, (g + 1) * GROUP)]
        picker.add(index, table[g], local)
    field_ref[...] = dot(p2m_ref[...], local[:order].astype(BF16), TN)
    copies[4].wait()
    classes = coarse_ref.shape[0]
    wide[0] = coarse[:, :128].astype(F32)
    wide[1, :, : order - 128] = coarse[:, 128:].astype(F32)
    for c in range(classes):
        rows = [wide[half, pl.ds(c, order, stride=classes), :] for half in range(2)]
        coarse_ref[c] = jnp.concatenate(rows, axis=1)[:, :order].astype(BF16)


def near_kernel(
    own_ref, low_ref, high_ref, list_ref, joined_ref, near_ref, field_ref, out_ref, window, table,
):
    picker = Picker(own_ref, low_ref, high_ref, window)
    width = near_ref.shape[1]
    classes = list_ref.shape[0]
    joined = joined_ref[...]
    out_ref[...] = field_ref[...]
    for g in range(0, classes, GROUP):
        members = range(g, min(g + GROUP, classes))
        for c in members:
            table[:, (c - g) * width : (c - g + 1) * width] = dot(near_ref[c], joined, NT).astype(BF16)
        index = [list_ref[c : c + 1, :] for c in members]
        picker.add(index, table[:, : len(members) * width], out_ref)


def downward_kernel(
    field_ref, slab_ref, low_ref, high_ref, list_ref, payload_ref, joined_ref, table_ref, m2l_ref,
    out_ref, down,
):
    order = m2l_ref.shape[1]
    classes, coarse = list_ref.shape
    span = out_ref.shape[0]
    index = jnp.transpose(list_ref[...])
    window = jnp.concatenate([low_ref[...], slab_ref[...], high_ref[...]], axis=0)
    spot = lax.broadcasted_iota(jnp.int32, (coarse, window.shape[0]), 1)
    hot = jnp.concatenate(
        [jnp.where(index[:, c : c + 1] == spot, 1.0, 0.0).astype(BF16) for c in range(classes)], axis=0
    )
    picked = dot(hot, window).astype(BF16)
    total = jnp.zeros((coarse, order), F32)
    for c in range(classes):
        total = total + dot(picked[c * coarse : (c + 1) * coarse, :order], m2l_ref[c], NT)
    local = total.astype(BF16)
    for j in range(8):
        down[pl.ds(j, coarse, stride=8), :] = dot(local, table_ref[j, :order])
    field = (field_ref[...] + jnp.transpose(down[...])).astype(BF16)
    by_kind = dot(joined_ref[...], field)
    kind = payload_ref[span : span + 1, :].astype(F32)
    tested = jnp.zeros(out_ref.shape, F32)
    for k in range(4):
        tested = jnp.where(kind == k, by_kind[k * span : (k + 1) * span], tested)
    out_ref[...] = tested.astype(BF16)


def call(kernel, outs, scratch, args, flops, megabytes, in_hbm=()):
    args = [
        pltpu.with_memory_space_constraint(x, pltpu.HBM) if i in in_hbm else x
        for i, x in enumerate(args)
    ]
    return pl.pallas_call(
        kernel,
        out_shape=outs,
        in_specs=[
            pl.BlockSpec(memory_space=pltpu.HBM if i in in_hbm else pltpu.VMEM)
            for i in range(len(args))
        ],
        out_specs=jax.tree.map(lambda _: pl.BlockSpec(memory_space=pltpu.VMEM), outs),
        scratch_shapes=scratch,
        compiler_params=pltpu.CompilerParams(vmem_limit_bytes=40 * 1024 * 1024),
        cost_estimate=pl.CostEstimate(
            flops=flops, bytes_accessed=int(megabytes * 1e6), transcendentals=0
        ),
    )(*args)


def shifted(block, axis, step):
    count = lax.axis_size(axis)
    return lax.ppermute(block, axis, [(i, i + step) for i in range(count) if 0 <= i + step < count])


def body(
    dual_coeffs, refine_select, refine_tiles, near_list, near_tiles, leaf_list, p2m, m2m, leaf_m2l,
    coarse_list, coarse_m2l,
):
    span, boxes = dual_coeffs.shape
    order, width = p2m.shape
    coarse = boxes // 8
    subs = lax.axis_size("sub")
    joined = jnp.transpose(refine_tiles, (0, 2, 1)).reshape(4 * span, width)
    m2m_rows = jnp.transpose(m2m, (1, 0, 2)).reshape(-1, order)
    leaf_rows = jnp.transpose(leaf_m2l, (1, 0, 2)).reshape(-1, order)
    coarse_rows = jnp.transpose(coarse_m2l, (1, 0, 2)).reshape(-1, order)
    payload, mine, table = call(
        upward_kernel,
        (
            jax.ShapeDtypeStruct((span + 8, boxes), BF16),
            jax.ShapeDtypeStruct((subs, coarse, 256), BF16),
            jax.ShapeDtypeStruct((8, 176, width), BF16),
        ),
        [pltpu.VMEM(a.shape, a.dtype) for a in (dual_coeffs, refine_select, joined, p2m, m2m_rows)]
        + [
            pltpu.VMEM((8 * order, width), F32),
            pltpu.VMEM((boxes, width), F32),
            pltpu.SemaphoreType.DMA((5,)),
        ],
        (dual_coeffs, refine_select, joined, p2m, m2m_rows),
        100_000_000, 1.0, (0, 1, 2, 3, 4),
    )
    low = shifted(payload, ("grp", "sub"), 1)
    high = shifted(payload, ("grp", "sub"), -1)
    slab = lax.all_to_all(mine, "sub", 0, 0).reshape(subs * coarse, 256)
    windows = (payload, low, high)
    leaf_args = (leaf_list.T, joined, p2m, leaf_rows, coarse_rows)
    leaf_field, coarse_table = call(
        leaf_kernel,
        (jax.ShapeDtypeStruct((width, boxes), F32), jax.ShapeDtypeStruct(coarse_m2l.shape, BF16)),
        [pltpu.VMEM(a.shape, a.dtype) for a in leaf_args]
        + [
            pltpu.VMEM((5 * (span + 8), 256), BF16),
            pltpu.VMEM((leaf_m2l.shape[0] // GROUP, 176, GROUP * width), BF16),
            pltpu.VMEM((leaf_rows.shape[0], width), F32),
            pltpu.VMEM((2, coarse_rows.shape[0], 128), F32),
            pltpu.VMEM((176, boxes), F32),
            pltpu.SemaphoreType.DMA((5,)),
        ],
        (*windows, *leaf_args),
        100_000_000, 1.0, (3, 4, 5, 6, 7),
    )
    slab_low = shifted(slab, "grp", 1)
    slab_high = shifted(slab, "grp", -1)
    field = call(
        near_kernel,
        jax.ShapeDtypeStruct((width, boxes), F32),
        [pltpu.VMEM((5 * (span + 8), 256), BF16), pltpu.VMEM((width, GROUP * width), BF16)],
        (*windows, near_list.T, joined, near_tiles, leaf_field),
        3_000_000_000, 2.0,
    )
    return call(
        downward_kernel,
        jax.ShapeDtypeStruct((span, boxes), BF16),
        [pltpu.VMEM((boxes, width), F32)],
        (
            field, slab, slab_low, slab_high, coarse_list.T, payload, joined, table, coarse_table,
        ),
        1_000_000_000, 3.0,
    )


def solution(mesh):
    placed = (
        P(None, ("grp", "sub")),
        P(("grp", "sub")),
        P(),
        P(("grp", "sub"), None),
        P(),
        P(("grp", "sub"), None),
        P(),
        P(),
        P(),
        P(("grp", "sub"), None),
        P(),
    )
    return jax.shard_map(
        body, mesh=mesh, in_specs=placed, out_specs=P(None, ("grp", "sub")), check_vma=False
    )
```

```python
import jax
import jax.numpy as jnp
from jax import lax
from jax.experimental import pallas as pl
from jax.experimental.pallas import tpu as pltpu
from jax.sharding import PartitionSpec as P

GROUP = 8
F32 = jnp.float32
BF16 = jnp.bfloat16
NT = (((1,), (1,)), ((), ()))
TN = (((0,), (0,)), ((), ()))


def dot(a, b, dims=(((1,), (0,)), ((), ()))):
    return lax.dot_general(a, b, dims, preferred_element_type=F32)


def refine_rows(payload, joined):
    span = joined.shape[0] // 4
    values = payload[:span, :].astype(F32)
    kind = payload[span : span + 1, :].astype(F32)
    spread = jnp.concatenate([jnp.where(kind == k, values, 0.0) for k in range(4)], axis=0)
    return dot(jnp.transpose(spread).astype(BF16), joined).astype(BF16)


def fetch(sources, targets, sems):
    copies = [
        pltpu.make_async_copy(source, target, sems.at[i])
        for i, (source, target) in enumerate(zip(sources, targets))
    ]
    for copy in copies:
        copy.start()
    return copies


def upward_kernel(
    dual_hbm, select_hbm, joined_hbm, p2m_hbm, m2m_hbm, payload_ref, out_ref, table_ref,
    dual, select, joined, p2m, m2m, product, refined, sems,
):
    copies = fetch(
        (dual_hbm, select_hbm, joined_hbm, p2m_hbm, m2m_hbm), (dual, select, joined, p2m, m2m), sems
    )
    subs, coarse, _ = out_ref.shape
    order, width = p2m.shape
    span, boxes = dual.shape
    out_ref[...] = jnp.zeros_like(out_ref)
    for copy in copies:
        copy.wait()
    payload_ref[:span] = dual[...]
    kind = select[...].reshape(1, boxes)
    payload_ref[span:] = jnp.broadcast_to(kind, (8, boxes)).astype(F32).astype(BF16)
    product[...] = dot(m2m[...], p2m[...])
    refined[...] = refine_rows(payload_ref[...], joined[...]).astype(F32)
    total = jnp.zeros((coarse, order), F32)
    for j in range(0, 8, 2):
        tables, rows = [], []
        for i in (j, j + 1):
            table = product[pl.ds(i, order, stride=8), :].astype(BF16)
            table_ref[i, :order] = table
            tables.append(table)
            rows.append(refined[pl.ds(i, coarse, stride=8), :].astype(BF16))
        total = total + dot(jnp.concatenate(rows, axis=1), jnp.concatenate(tables, axis=1), NT)
    for d in range(subs):
        out_ref[d, :, :order] = total.astype(BF16)


class Picker:
    def __init__(self, own_ref, low_ref, high_ref, window):
        self.depth, self.boxes = own_ref.shape
        self.window = window
        whole = jnp.concatenate(
            [low_ref[...], own_ref[...], high_ref[...], jnp.zeros((self.depth, 128), BF16)], axis=1
        ).astype(F32)
        self.blocks = whole.shape[1] // 256
        window[...] = jnp.concatenate(
            [whole[:, b * 256 : (b + 1) * 256] for b in range(self.blocks)], axis=0
        ).astype(BF16)
        self.spot = lax.broadcasted_iota(jnp.int32, (256, self.boxes), 0).astype(BF16)

    def hot(self, index):
        low = (index & 255).astype(F32).astype(BF16)
        return jnp.where(low == self.spot, jnp.array(1.0, BF16), jnp.array(0.0, BF16))

    def expand(self, index, got):
        block, depth = index >> 8, self.depth
        value = jnp.zeros((depth, self.boxes), F32)
        for b in range(self.blocks):
            value = jnp.where(block == b, got[b * depth : (b + 1) * depth], value)
        kind = value[depth - 8 : depth - 7]
        return [jnp.where(kind == k, value[: depth - 8], 0.0) for k in range(4)]

    def add(self, index, table, out):
        boxes = self.boxes
        got = dot(self.window[...], jnp.concatenate([self.hot(i) for i in index], axis=1))
        parts = []
        for c, i in enumerate(index):
            parts += self.expand(i, got[:, c * boxes : (c + 1) * boxes])
        out[...] += dot(table, jnp.concatenate(parts, axis=0).astype(BF16))


def table_kernel(
    joined_hbm, p2m_hbm, m2l_hbm, coarse_hbm, leaf_ref, coarse_ref, joined, p2m, m2l, coarse, product, wide, sems
):
    copies = fetch((joined_hbm, p2m_hbm, m2l_hbm, coarse_hbm), (joined, p2m, m2l, coarse), sems)
    order, width = p2m.shape
    copies[0].wait()
    copies[1].wait()
    spread = dot(p2m[...], joined[...], NT).astype(BF16)
    copies[2].wait()
    product[...] = dot(m2l[...], spread)
    classes = leaf_ref.shape[0] * GROUP
    for c in range(classes):
        at = slice((c % GROUP) * width, (c % GROUP + 1) * width)
        leaf_ref[c // GROUP, :order, at] = product[pl.ds(c, order, stride=classes), :].astype(BF16)
    copies[3].wait()
    classes = coarse_ref.shape[0]
    wide[0] = coarse[:, :128].astype(F32)
    wide[1, :, : order - 128] = coarse[:, 128:].astype(F32)
    for c in range(classes):
        rows = [wide[half, pl.ds(c, order, stride=classes), :] for half in range(2)]
        coarse_ref[c] = jnp.concatenate(rows, axis=1)[:, :order].astype(BF16)


def leaf_kernel(own_ref, low_ref, high_ref, list_ref, p2m_ref, table_ref, field_ref, window, local):
    picker = Picker(own_ref, low_ref, high_ref, window)
    order = p2m_ref.shape[0]
    local[...] = jnp.zeros_like(local)
    for g in range(table_ref.shape[0]):
        index = [list_ref[c : c + 1, :] for c in range(g * GROUP, (g + 1) * GROUP)]
        picker.add(index, table_ref[g], local)
    field_ref[...] = dot(p2m_ref[...], local[:order].astype(BF16), TN)


def near_kernel(
    own_ref, low_ref, high_ref, list_ref, joined_ref, near_ref, field_ref, out_ref, window, table,
):
    picker = Picker(own_ref, low_ref, high_ref, window)
    width = near_ref.shape[1]
    classes = list_ref.shape[0]
    joined = joined_ref[...]
    out_ref[...] = field_ref[...]
    for g in range(0, classes, GROUP):
        members = range(g, min(g + GROUP, classes))
        for c in members:
            table[:, (c - g) * width : (c - g + 1) * width] = dot(near_ref[c], joined, NT).astype(BF16)
        index = [list_ref[c : c + 1, :] for c in members]
        picker.add(index, table[:, : len(members) * width], out_ref)


def downward_kernel(
    field_ref, slab_ref, low_ref, high_ref, list_ref, payload_ref, joined_ref, table_ref, m2l_ref,
    out_ref, down,
):
    order = m2l_ref.shape[1]
    classes, coarse = list_ref.shape
    span = out_ref.shape[0]
    index = jnp.transpose(list_ref[...])
    window = jnp.concatenate([low_ref[...], slab_ref[...], high_ref[...]], axis=0)
    spot = lax.broadcasted_iota(jnp.int32, (coarse, window.shape[0]), 1)
    hot = jnp.concatenate(
        [jnp.where(index[:, c : c + 1] == spot, 1.0, 0.0).astype(BF16) for c in range(classes)], axis=0
    )
    picked = dot(hot, window).astype(BF16)
    total = jnp.zeros((coarse, order), F32)
    for c in range(classes):
        total = total + dot(picked[c * coarse : (c + 1) * coarse, :order], m2l_ref[c], NT)
    local = total.astype(BF16)
    for j in range(8):
        down[pl.ds(j, coarse, stride=8), :] = dot(local, table_ref[j, :order])
    field = (field_ref[...] + jnp.transpose(down[...])).astype(BF16)
    by_kind = dot(joined_ref[...], field)
    kind = payload_ref[span : span + 1, :].astype(F32)
    tested = jnp.zeros(out_ref.shape, F32)
    for k in range(4):
        tested = jnp.where(kind == k, by_kind[k * span : (k + 1) * span], tested)
    out_ref[...] = tested.astype(BF16)


def call(kernel, outs, scratch, args, flops, megabytes, in_hbm=()):
    args = [
        pltpu.with_memory_space_constraint(x, pltpu.HBM) if i in in_hbm else x
        for i, x in enumerate(args)
    ]
    return pl.pallas_call(
        kernel,
        out_shape=outs,
        in_specs=[
            pl.BlockSpec(memory_space=pltpu.HBM if i in in_hbm else pltpu.VMEM)
            for i in range(len(args))
        ],
        out_specs=jax.tree.map(lambda _: pl.BlockSpec(memory_space=pltpu.VMEM), outs),
        scratch_shapes=scratch,
        compiler_params=pltpu.CompilerParams(vmem_limit_bytes=40 * 1024 * 1024),
        cost_estimate=pl.CostEstimate(
            flops=flops, bytes_accessed=int(megabytes * 1e6), transcendentals=0
        ),
    )(*args)


def shifted(block, axis, step):
    count = lax.axis_size(axis)
    return lax.ppermute(block, axis, [(i, i + step) for i in range(count) if 0 <= i + step < count])


def body(
    dual_coeffs, refine_select, refine_tiles, near_list, near_tiles, leaf_list, p2m, m2m, leaf_m2l,
    coarse_list, coarse_m2l,
):
    span, boxes = dual_coeffs.shape
    order, width = p2m.shape
    coarse = boxes // 8
    subs = lax.axis_size("sub")
    joined = jnp.transpose(refine_tiles, (0, 2, 1)).reshape(4 * span, width)
    m2m_rows = jnp.transpose(m2m, (1, 0, 2)).reshape(-1, order)
    leaf_rows = jnp.transpose(leaf_m2l, (1, 0, 2)).reshape(-1, order)
    coarse_rows = jnp.transpose(coarse_m2l, (1, 0, 2)).reshape(-1, order)
    payload, mine, table = call(
        upward_kernel,
        (
            jax.ShapeDtypeStruct((span + 8, boxes), BF16),
            jax.ShapeDtypeStruct((subs, coarse, 256), BF16),
            jax.ShapeDtypeStruct((8, 176, width), BF16),
        ),
        [pltpu.VMEM(a.shape, a.dtype) for a in (dual_coeffs, refine_select, joined, p2m, m2m_rows)]
        + [
            pltpu.VMEM((8 * order, width), F32),
            pltpu.VMEM((boxes, width), F32),
            pltpu.SemaphoreType.DMA((5,)),
        ],
        (dual_coeffs, refine_select, joined, p2m, m2m_rows),
        100_000_000, 1.0, (0, 1, 2, 3, 4),
    )
    low = shifted(payload, ("grp", "sub"), 1)
    high = shifted(payload, ("grp", "sub"), -1)
    slab = lax.all_to_all(mine, "sub", 0, 0).reshape(subs * coarse, 256)
    windows = (payload, low, high)
    table_args = (joined, p2m, leaf_rows, coarse_rows)
    leaf_table, coarse_table = call(
        table_kernel,
        (
            jax.ShapeDtypeStruct((leaf_m2l.shape[0] // GROUP, 176, GROUP * width), BF16),
            jax.ShapeDtypeStruct(coarse_m2l.shape, BF16),
        ),
        [pltpu.VMEM(a.shape, a.dtype) for a in table_args]
        + [
            pltpu.VMEM((leaf_rows.shape[0], width), F32),
            pltpu.VMEM((2, coarse_rows.shape[0], 128), F32),
            pltpu.SemaphoreType.DMA((4,)),
        ],
        table_args,
        100_000_000, 1.0, (0, 1, 2, 3),
    )
    leaf_field = call(
        leaf_kernel,
        jax.ShapeDtypeStruct((width, boxes), F32),
        [pltpu.VMEM((5 * (span + 8), 256), BF16), pltpu.VMEM((176, boxes), F32)],
        (*windows, leaf_list.T, p2m, leaf_table),
        100_000_000, 1.0,
    )
    slab_low = shifted(slab, "grp", 1)
    slab_high = shifted(slab, "grp", -1)
    field = call(
        near_kernel,
        jax.ShapeDtypeStruct((width, boxes), F32),
        [pltpu.VMEM((5 * (span + 8), 256), BF16), pltpu.VMEM((width, GROUP * width), BF16)],
        (*windows, near_list.T, joined, near_tiles, leaf_field),
        3_000_000_000, 2.0,
    )
    return call(
        downward_kernel,
        jax.ShapeDtypeStruct((span, boxes), BF16),
        [pltpu.VMEM((boxes, width), F32)],
        (
            field, slab, slab_low, slab_high, coarse_list.T, payload, joined, table, coarse_table,
        ),
        1_000_000_000, 3.0,
    )


def solution(mesh):
    placed = (
        P(None, ("grp", "sub")),
        P(("grp", "sub")),
        P(),
        P(("grp", "sub"), None),
        P(),
        P(("grp", "sub"), None),
        P(),
        P(),
        P(),
        P(("grp", "sub"), None),
        P(),
    )
    return jax.shard_map(
        body, mesh=mesh, in_specs=placed, out_specs=P(None, ("grp", "sub")), check_vma=False
    )
```

```python
import jax
import jax.numpy as jnp
from jax import lax
from jax.experimental import pallas as pl
from jax.experimental.pallas import tpu as pltpu
from jax.sharding import PartitionSpec as P

GROUP = 8
F32 = jnp.float32
BF16 = jnp.bfloat16
NT = (((1,), (1,)), ((), ()))
TN = (((0,), (0,)), ((), ()))


def dot(a, b, dims=(((1,), (0,)), ((), ()))):
    return lax.dot_general(a, b, dims, preferred_element_type=F32)


def refine_rows(payload, joined):
    span = joined.shape[0] // 4
    values = payload[:span, :].astype(F32)
    kind = payload[span : span + 1, :].astype(F32)
    spread = jnp.concatenate([jnp.where(kind == k, values, 0.0) for k in range(4)], axis=0)
    return dot(jnp.transpose(spread).astype(BF16), joined).astype(BF16)


def fetch(sources, targets, sems):
    copies = [
        pltpu.make_async_copy(source, target, sems.at[i])
        for i, (source, target) in enumerate(zip(sources, targets))
    ]
    for copy in copies:
        copy.start()
    return copies


def upward_kernel(
    dual_hbm, select_hbm, joined_hbm, p2m_hbm, m2m_hbm, payload_ref, out_ref, table_ref,
    dual, select, joined, p2m, m2m, product, refined, sems,
):
    copies = fetch(
        (dual_hbm, select_hbm, joined_hbm, p2m_hbm, m2m_hbm), (dual, select, joined, p2m, m2m), sems
    )
    subs, coarse, _ = out_ref.shape
    order, width = p2m.shape
    span, boxes = dual.shape
    out_ref[...] = jnp.zeros_like(out_ref)
    for copy in copies:
        copy.wait()
    payload_ref[:span] = dual[...]
    kind = select[...].reshape(1, boxes)
    payload_ref[span:] = jnp.broadcast_to(kind, (8, boxes)).astype(F32).astype(BF16)
    product[...] = dot(m2m[...], p2m[...])
    refined[...] = refine_rows(payload_ref[...], joined[...]).astype(F32)
    total = jnp.zeros((coarse, order), F32)
    for j in range(0, 8, 2):
        tables, rows = [], []
        for i in (j, j + 1):
            table = product[pl.ds(i, order, stride=8), :].astype(BF16)
            table_ref[i, :order] = table
            tables.append(table)
            rows.append(refined[pl.ds(i, coarse, stride=8), :].astype(BF16))
        total = total + dot(jnp.concatenate(rows, axis=1), jnp.concatenate(tables, axis=1), NT)
    for d in range(subs):
        out_ref[d, :, :order] = total.astype(BF16)


class Picker:
    def __init__(self, own_ref, low_ref, high_ref, window):
        self.depth, self.boxes = own_ref.shape
        self.window = window
        whole = jnp.concatenate(
            [low_ref[...], own_ref[...], high_ref[...], jnp.zeros((self.depth, 128), BF16)], axis=1
        ).astype(F32)
        self.blocks = whole.shape[1] // 256
        window[...] = jnp.concatenate(
            [whole[:, b * 256 : (b + 1) * 256] for b in range(self.blocks)], axis=0
        ).astype(BF16)
        self.spot = lax.broadcasted_iota(jnp.int32, (256, self.boxes), 0).astype(BF16)

    def hot(self, index):
        low = (index & 255).astype(F32).astype(BF16)
        return jnp.where(low == self.spot, jnp.array(1.0, BF16), jnp.array(0.0, BF16))

    def expand(self, index, got):
        block, depth = index >> 8, self.depth
        value = jnp.zeros((depth, self.boxes), F32)
        for b in range(self.blocks):
            value = jnp.where(block == b, got[b * depth : (b + 1) * depth], value)
        kind = value[depth - 8 : depth - 7]
        return [jnp.where(kind == k, value[: depth - 8], 0.0) for k in range(4)]

    def add(self, index, table, out):
        boxes = self.boxes
        got = dot(self.window[...], jnp.concatenate([self.hot(i) for i in index], axis=1))
        parts = []
        for c, i in enumerate(index):
            parts += self.expand(i, got[:, c * boxes : (c + 1) * boxes])
        out[...] += dot(table, jnp.concatenate(parts, axis=0).astype(BF16))


def by_eights(ref, rows, classes):
    order, width = rows.shape[0] // classes, rows.shape[1]
    split = rows.reshape(order, classes // 8, 8, width)
    for b in range(classes // 8):
        ref[b, :, :width] = split[:, b].reshape(order * 8, width)


def table_kernel(joined_ref, p2m_ref, m2l_ref, out_ref, product):
    order, width = p2m_ref.shape
    classes = out_ref.shape[0] * GROUP
    spread = dot(p2m_ref[...], joined_ref[...], NT).astype(BF16)
    by_eights(product, dot(m2l_ref[...], spread), classes)
    for c in range(classes):
        at = slice((c % GROUP) * width, (c % GROUP + 1) * width)
        rows = product[c // 8, pl.ds(c % 8, order, stride=8), :]
        out_ref[c // GROUP, :order, at] = rows.astype(BF16)


def leaf_kernel(own_ref, low_ref, high_ref, list_ref, p2m_ref, table_ref, field_ref, window, local):
    picker = Picker(own_ref, low_ref, high_ref, window)
    order = p2m_ref.shape[0]
    local[...] = jnp.zeros_like(local)
    for g in range(table_ref.shape[0]):
        index = [list_ref[c : c + 1, :] for c in range(g * GROUP, (g + 1) * GROUP)]
        picker.add(index, table_ref[g], local)
    field_ref[...] = dot(p2m_ref[...], local[:order].astype(BF16), TN)


def near_kernel(
    own_ref, low_ref, high_ref, list_ref, joined_ref, near_ref, field_ref, coarse, out_ref, coarse_ref,
    window, table, wide,
):
    picker = Picker(own_ref, low_ref, high_ref, window)
    width = near_ref.shape[1]
    classes = list_ref.shape[0]
    joined = joined_ref[...]
    out_ref[...] = field_ref[...]
    for g in range(0, classes, GROUP):
        members = range(g, min(g + GROUP, classes))
        for c in members:
            table[:, (c - g) * width : (c - g + 1) * width] = dot(near_ref[c], joined, NT).astype(BF16)
        index = [list_ref[c : c + 1, :] for c in members]
        picker.add(index, table[:, : len(members) * width], out_ref)
    classes, order, _ = coarse_ref.shape
    by_eights(wide.at[0], coarse[:, :128].astype(F32), classes)
    by_eights(wide.at[1], coarse[:, 128:].astype(F32), classes)
    for c in range(classes):
        rows = [wide[half, c // 8, pl.ds(c % 8, order, stride=8), :] for half in range(2)]
        coarse_ref[c] = jnp.concatenate(rows, axis=1)[:, :order].astype(BF16)


def downward_kernel(
    field_ref, slab_ref, low_ref, high_ref, list_ref, payload_ref, joined_ref, table_ref, m2l_ref,
    out_ref, down,
):
    order = m2l_ref.shape[1]
    classes, coarse = list_ref.shape
    span = out_ref.shape[0]
    index = jnp.transpose(list_ref[...])
    window = jnp.concatenate([low_ref[...], slab_ref[...], high_ref[...]], axis=0)
    spot = lax.broadcasted_iota(jnp.int32, (coarse, window.shape[0]), 1)
    hot = jnp.concatenate(
        [jnp.where(index[:, c : c + 1] == spot, 1.0, 0.0).astype(BF16) for c in range(classes)], axis=0
    )
    picked = dot(hot, window).astype(BF16)
    total = jnp.zeros((coarse, order), F32)
    for c in range(classes):
        total = total + dot(picked[c * coarse : (c + 1) * coarse, :order], m2l_ref[c], NT)
    local = total.astype(BF16)
    for j in range(8):
        down[pl.ds(j, coarse, stride=8), :] = dot(local, table_ref[j, :order])
    field = (field_ref[...] + jnp.transpose(down[...])).astype(BF16)
    by_kind = dot(joined_ref[...], field)
    kind = payload_ref[span : span + 1, :].astype(F32)
    tested = jnp.zeros(out_ref.shape, F32)
    for k in range(4):
        tested = jnp.where(kind == k, by_kind[k * span : (k + 1) * span], tested)
    out_ref[...] = tested.astype(BF16)


def call(kernel, outs, scratch, args, flops, megabytes, in_hbm=()):
    args = [
        pltpu.with_memory_space_constraint(x, pltpu.HBM) if i in in_hbm else x
        for i, x in enumerate(args)
    ]
    return pl.pallas_call(
        kernel,
        out_shape=outs,
        in_specs=[
            pl.BlockSpec(memory_space=pltpu.HBM if i in in_hbm else pltpu.VMEM)
            for i in range(len(args))
        ],
        out_specs=jax.tree.map(lambda _: pl.BlockSpec(memory_space=pltpu.VMEM), outs),
        scratch_shapes=scratch,
        compiler_params=pltpu.CompilerParams(vmem_limit_bytes=32 * 1024 * 1024),
        cost_estimate=pl.CostEstimate(
            flops=flops, bytes_accessed=int(megabytes * 1e6), transcendentals=0
        ),
    )(*args)


def shifted(block, axis, step):
    count = lax.axis_size(axis)
    return lax.ppermute(block, axis, [(i, i + step) for i in range(count) if 0 <= i + step < count])


def body(
    dual_coeffs, refine_select, refine_tiles, near_list, near_tiles, leaf_list, p2m, m2m, leaf_m2l,
    coarse_list, coarse_m2l,
):
    span, boxes = dual_coeffs.shape
    order, width = p2m.shape
    coarse = boxes // 8
    subs = lax.axis_size("sub")
    joined = jnp.transpose(refine_tiles, (0, 2, 1)).reshape(4 * span, width)
    m2m_rows = jnp.transpose(m2m, (1, 0, 2)).reshape(-1, order)
    leaf_rows = jnp.transpose(leaf_m2l, (1, 0, 2)).reshape(-1, order)
    coarse_rows = jnp.transpose(coarse_m2l, (1, 0, 2)).reshape(-1, order)
    payload, mine, table = call(
        upward_kernel,
        (
            jax.ShapeDtypeStruct((span + 8, boxes), BF16),
            jax.ShapeDtypeStruct((subs, coarse, 256), BF16),
            jax.ShapeDtypeStruct((8, 176, width), BF16),
        ),
        [pltpu.VMEM(a.shape, a.dtype) for a in (dual_coeffs, refine_select, joined, p2m, m2m_rows)]
        + [
            pltpu.VMEM((8 * order, width), F32),
            pltpu.VMEM((boxes, width), F32),
            pltpu.SemaphoreType.DMA((5,)),
        ],
        (dual_coeffs, refine_select, joined, p2m, m2m_rows),
        10_000_000_000, 1.0, (0, 1, 2, 3, 4),
    )
    low = shifted(payload, ("grp", "sub"), 1)
    high = shifted(payload, ("grp", "sub"), -1)
    slab = lax.all_to_all(mine, "sub", 0, 0).reshape(subs * coarse, 256)
    windows = (payload, low, high)
    leaf_table = call(
        table_kernel,
        jax.ShapeDtypeStruct((leaf_m2l.shape[0] // GROUP, 176, GROUP * width), BF16),
        [pltpu.VMEM((leaf_m2l.shape[0] // 8, 8 * order, width), F32)],
        (joined, p2m, leaf_rows),
        100_000_000, 1.0,
    )
    leaf_field = call(
        leaf_kernel,
        jax.ShapeDtypeStruct((width, boxes), F32),
        [pltpu.VMEM((5 * (span + 8), 256), BF16), pltpu.VMEM((176, boxes), F32)],
        (*windows, leaf_list.T, p2m, leaf_table),
        2_000_000_000, 1.0,
    )
    slab_low = shifted(slab, "grp", 1)
    slab_high = shifted(slab, "grp", -1)
    field, coarse_table = call(
        near_kernel,
        (jax.ShapeDtypeStruct((width, boxes), F32), jax.ShapeDtypeStruct(coarse_m2l.shape, BF16)),
        [
            pltpu.VMEM((5 * (span + 8), 256), BF16),
            pltpu.VMEM((width, GROUP * width), BF16),
            pltpu.VMEM((2, coarse_m2l.shape[0] // 8, 8 * order, 128), F32),
        ],
        (*windows, near_list.T, joined, near_tiles, leaf_field, coarse_rows),
        3_000_000_000, 2.0,
    )
    return call(
        downward_kernel,
        jax.ShapeDtypeStruct((span, boxes), BF16),
        [pltpu.VMEM((boxes, width), F32)],
        (
            field, slab, slab_low, slab_high, coarse_list.T, payload, joined, table, coarse_table,
        ),
        1_000_000_000, 3.0,
    )


def solution(mesh):
    placed = (
        P(None, ("grp", "sub")),
        P(("grp", "sub")),
        P(),
        P(("grp", "sub"), None),
        P(),
        P(("grp", "sub"), None),
        P(),
        P(),
        P(),
        P(("grp", "sub"), None),
        P(),
    )
    return jax.shard_map(
        body, mesh=mesh, in_specs=placed, out_specs=P(None, ("grp", "sub")), check_vma=False
    )
```

```python
import jax
import jax.numpy as jnp
from jax import lax
from jax.experimental import pallas as pl
from jax.experimental.pallas import tpu as pltpu
from jax.sharding import PartitionSpec as P

LEAF_GROUP = 8
NEAR_GROUP = 14
F32 = jnp.float32
BF16 = jnp.bfloat16
NT = (((1,), (1,)), ((), ()))
TN = (((0,), (0,)), ((), ()))


def dot(a, b, dims=(((1,), (0,)), ((), ()))):
    return lax.dot_general(a, b, dims, preferred_element_type=F32)


def refine_rows(payload, joined):
    span = joined.shape[0] // 4
    values = payload[:span, :].astype(F32)
    kind = payload[span : span + 1, :].astype(F32)
    spread = jnp.concatenate([jnp.where(kind == k, values, 0.0) for k in range(4)], axis=0)
    return dot(jnp.transpose(spread).astype(BF16), joined).astype(BF16)


def fetch(sources, targets, sems):
    copies = [
        pltpu.make_async_copy(source, target, sems.at[i])
        for i, (source, target) in enumerate(zip(sources, targets))
    ]
    for copy in copies:
        copy.start()
    return copies


def upward_kernel(
    dual_hbm, select_hbm, joined_hbm, p2m_hbm, m2m_hbm, payload_ref, out_ref, table_ref,
    dual, select, joined, p2m, m2m, product, refined, sems,
):
    copies = fetch(
        (dual_hbm, select_hbm, joined_hbm, p2m_hbm, m2m_hbm), (dual, select, joined, p2m, m2m), sems
    )
    subs, coarse, _ = out_ref.shape
    order, width = p2m.shape
    span, boxes = dual.shape
    out_ref[...] = jnp.zeros_like(out_ref)
    for copy in copies:
        copy.wait()
    payload_ref[:span] = dual[...]
    kind = select[...].reshape(1, boxes)
    payload_ref[span:] = jnp.broadcast_to(kind, (8, boxes)).astype(F32).astype(BF16)
    product[...] = dot(m2m[...], p2m[...])
    refined[...] = refine_rows(payload_ref[...], joined[...]).astype(F32)
    total = jnp.zeros((coarse, order), F32)
    for j in range(0, 8, 2):
        tables, rows = [], []
        for i in (j, j + 1):
            table = product[pl.ds(i, order, stride=8), :].astype(BF16)
            table_ref[:order, i * width : (i + 1) * width] = table
            tables.append(table)
            rows.append(refined[pl.ds(i, coarse, stride=8), :].astype(BF16))
        total = total + dot(jnp.concatenate(rows, axis=1), jnp.concatenate(tables, axis=1), NT)
    for d in range(subs):
        out_ref[d, :, :order] = total.astype(BF16)


class Picker:
    def __init__(self, own_ref, low_ref, high_ref, window):
        self.depth, self.boxes = own_ref.shape
        self.window = window
        whole = jnp.concatenate(
            [low_ref[...], own_ref[...], high_ref[...], jnp.zeros((self.depth, 128), BF16)], axis=1
        ).astype(F32)
        self.blocks = whole.shape[1] // 256
        window[...] = jnp.concatenate(
            [whole[:, b * 256 : (b + 1) * 256] for b in range(self.blocks)], axis=0
        ).astype(BF16)
        self.spot = lax.broadcasted_iota(jnp.int32, (256, self.boxes), 0).astype(BF16)

    def hot(self, index):
        low = (index & 255).astype(F32).astype(BF16)
        return jnp.where(low == self.spot, jnp.array(1.0, BF16), jnp.array(0.0, BF16))

    def expand(self, index, got):
        block, depth = index >> 8, self.depth
        value = jnp.zeros((depth, self.boxes), F32)
        for b in range(self.blocks):
            value = jnp.where(block == b, got[b * depth : (b + 1) * depth], value)
        kind = value[depth - 8 : depth - 7]
        return [jnp.where(kind == k, value[: depth - 8], 0.0) for k in range(4)]

    def add(self, index, table, out):
        boxes = self.boxes
        got = dot(self.window[...], jnp.concatenate([self.hot(i) for i in index], axis=1))
        parts = []
        for c, i in enumerate(index):
            parts += self.expand(i, got[:, c * boxes : (c + 1) * boxes])
        out[...] += dot(table, jnp.concatenate(parts, axis=0).astype(BF16))


def by_eights(ref, rows, classes):
    order, width = rows.shape[0] // classes, rows.shape[1]
    split = rows.reshape(order, classes // 8, 8, width)
    for b in range(classes // 8):
        ref[b, :, :width] = split[:, b].reshape(order * 8, width)


def table_kernel(joined_ref, p2m_ref, m2l_ref, out_ref, product):
    order, width = p2m_ref.shape
    classes = out_ref.shape[0] * LEAF_GROUP
    spread = dot(p2m_ref[...], joined_ref[...], NT).astype(BF16)
    by_eights(product, dot(m2l_ref[...], spread), classes)
    for c in range(classes):
        at = slice((c % LEAF_GROUP) * width, (c % LEAF_GROUP + 1) * width)
        rows = product[c // 8, pl.ds(c % 8, order, stride=8), :]
        out_ref[c // LEAF_GROUP, :order, at] = rows.astype(BF16)


def leaf_kernel(own_ref, low_ref, high_ref, list_ref, p2m_ref, table_ref, field_ref, window, local):
    picker = Picker(own_ref, low_ref, high_ref, window)
    order = p2m_ref.shape[0]
    local[...] = jnp.zeros_like(local)
    for g in range(table_ref.shape[0]):
        index = [list_ref[c : c + 1, :] for c in range(g * LEAF_GROUP, (g + 1) * LEAF_GROUP)]
        picker.add(index, table_ref[g], local)
    field_ref[...] = dot(p2m_ref[...], local[:order].astype(BF16), TN)


def near_kernel(
    own_ref, low_ref, high_ref, list_ref, joined_ref, near_ref, field_ref, coarse, out_ref, coarse_ref,
    window, table, wide,
):
    picker = Picker(own_ref, low_ref, high_ref, window)
    width = near_ref.shape[1]
    classes = list_ref.shape[0]
    joined = joined_ref[...]
    out_ref[...] = field_ref[...]
    for g in range(0, classes, NEAR_GROUP):
        members = range(g, min(g + NEAR_GROUP, classes))
        for c in members:
            at = (c - g) * width
            table[:, at : at + width] = dot(near_ref[c], joined, NT).astype(BF16)
        index = [list_ref[c : c + 1, :] for c in members]
        picker.add(index, table[:, : len(members) * width], out_ref)
    classes, order, _ = coarse_ref.shape
    by_eights(wide.at[0], coarse[:, :128].astype(F32), classes)
    by_eights(wide.at[1], coarse[:, 128:].astype(F32), classes)
    for c in range(classes):
        rows = [wide[half, c // 8, pl.ds(c % 8, order, stride=8), :] for half in range(2)]
        coarse_ref[c] = jnp.concatenate(rows, axis=1)[:, :order].astype(BF16)


def downward_kernel(
    field_ref, slab_ref, low_ref, high_ref, list_ref, payload_ref, joined_ref, table_ref, m2l_ref,
    out_ref, down,
):
    order = m2l_ref.shape[1]
    classes, coarse = list_ref.shape
    span = out_ref.shape[0]
    index = jnp.transpose(list_ref[...])
    window = jnp.concatenate([low_ref[...], slab_ref[...], high_ref[...]], axis=0)
    spot = lax.broadcasted_iota(jnp.int32, (coarse, window.shape[0]), 1)
    hot = jnp.concatenate(
        [jnp.where(index[:, c : c + 1] == spot, 1.0, 0.0).astype(BF16) for c in range(classes)], axis=0
    )
    count = hot.shape[0] // 4
    picked = jnp.concatenate(
        [dot(hot[i * count : (i + 1) * count], window).astype(BF16) for i in range(4)], axis=0
    )
    total = jnp.zeros((coarse, order), F32)
    for c in range(classes):
        total = total + dot(picked[c * coarse : (c + 1) * coarse, :order], m2l_ref[c], NT)
    local = total.astype(BF16)
    parts = dot(local, table_ref[:order])
    for j in range(8):
        down[pl.ds(j, coarse, stride=8), :] = parts[:, j * 128 : (j + 1) * 128]
    field = (field_ref[...] + jnp.transpose(down[...])).astype(BF16)
    by_kind = dot(joined_ref[...], field)
    kind = payload_ref[span : span + 1, :].astype(F32)
    tested = jnp.zeros(out_ref.shape, F32)
    for k in range(4):
        tested = jnp.where(kind == k, by_kind[k * span : (k + 1) * span], tested)
    out_ref[...] = tested.astype(BF16)


def call(kernel, outs, scratch, args, flops, megabytes, in_hbm=()):
    args = [
        pltpu.with_memory_space_constraint(x, pltpu.HBM) if i in in_hbm else x
        for i, x in enumerate(args)
    ]
    return pl.pallas_call(
        kernel,
        out_shape=outs,
        in_specs=[
            pl.BlockSpec(memory_space=pltpu.HBM if i in in_hbm else pltpu.VMEM)
            for i in range(len(args))
        ],
        out_specs=jax.tree.map(lambda _: pl.BlockSpec(memory_space=pltpu.VMEM), outs),
        scratch_shapes=scratch,
        compiler_params=pltpu.CompilerParams(vmem_limit_bytes=32 * 1024 * 1024),
        cost_estimate=pl.CostEstimate(
            flops=flops, bytes_accessed=int(megabytes * 1e6), transcendentals=0
        ),
    )(*args)


def shifted(block, axis, step):
    count = lax.axis_size(axis)
    return lax.ppermute(block, axis, [(i, i + step) for i in range(count) if 0 <= i + step < count])


def body(
    dual_coeffs, refine_select, refine_tiles, near_list, near_tiles, leaf_list, p2m, m2m, leaf_m2l,
    coarse_list, coarse_m2l,
):
    span, boxes = dual_coeffs.shape
    order, width = p2m.shape
    coarse = boxes // 8
    subs = lax.axis_size("sub")
    joined = jnp.transpose(refine_tiles, (0, 2, 1)).reshape(4 * span, width)
    m2m_rows = jnp.transpose(m2m, (1, 0, 2)).reshape(-1, order)
    leaf_rows = jnp.transpose(leaf_m2l, (1, 0, 2)).reshape(-1, order)
    coarse_rows = jnp.transpose(coarse_m2l, (1, 0, 2)).reshape(-1, order)
    payload, mine, table = call(
        upward_kernel,
        (
            jax.ShapeDtypeStruct((span + 8, boxes), BF16),
            jax.ShapeDtypeStruct((subs, coarse, 256), BF16),
            jax.ShapeDtypeStruct((176, 8 * width), BF16),
        ),
        [pltpu.VMEM(a.shape, a.dtype) for a in (dual_coeffs, refine_select, joined, p2m, m2m_rows)]
        + [
            pltpu.VMEM((8 * order, width), F32),
            pltpu.VMEM((boxes, width), F32),
            pltpu.SemaphoreType.DMA((5,)),
        ],
        (dual_coeffs, refine_select, joined, p2m, m2m_rows),
        10_000_000_000, 1.0, (0, 1, 2, 3, 4),
    )
    low = shifted(payload, ("grp", "sub"), 1)
    high = shifted(payload, ("grp", "sub"), -1)
    slab = lax.all_to_all(mine, "sub", 0, 0).reshape(subs * coarse, 256)
    windows = (payload, low, high)
    leaf_table = call(
        table_kernel,
        jax.ShapeDtypeStruct((leaf_m2l.shape[0] // LEAF_GROUP, 176, LEAF_GROUP * width), BF16),
        [pltpu.VMEM((leaf_m2l.shape[0] // 8, 8 * order, width), F32)],
        (joined, p2m, leaf_rows),
        100_000_000, 1.0,
    )
    leaf_field = call(
        leaf_kernel,
        jax.ShapeDtypeStruct((width, boxes), F32),
        [pltpu.VMEM((5 * (span + 8), 256), BF16), pltpu.VMEM((176, boxes), F32)],
        (*windows, leaf_list.T, p2m, leaf_table),
        2_000_000_000, 1.0,
    )
    slab_low = shifted(slab, "grp", 1)
    slab_high = shifted(slab, "grp", -1)
    field, coarse_table = call(
        near_kernel,
        (jax.ShapeDtypeStruct((width, boxes), F32), jax.ShapeDtypeStruct(coarse_m2l.shape, BF16)),
        [
            pltpu.VMEM((5 * (span + 8), 256), BF16),
            pltpu.VMEM((width, NEAR_GROUP * width), BF16),
            pltpu.VMEM((2, coarse_m2l.shape[0] // 8, 8 * order, 128), F32),
        ],
        (*windows, near_list.T, joined, near_tiles, leaf_field, coarse_rows),
        3_000_000_000, 2.0,
    )
    return call(
        downward_kernel,
        jax.ShapeDtypeStruct((span, boxes), BF16),
        [pltpu.VMEM((boxes, width), F32)],
        (
            field, slab, slab_low, slab_high, coarse_list.T, payload, joined, table, coarse_table,
        ),
        1_000_000_000, 3.0,
    )


def solution(mesh):
    placed = (
        P(None, ("grp", "sub")),
        P(("grp", "sub")),
        P(),
        P(("grp", "sub"), None),
        P(),
        P(("grp", "sub"), None),
        P(),
        P(),
        P(),
        P(("grp", "sub"), None),
        P(),
    )
    return jax.shard_map(
        body, mesh=mesh, in_specs=placed, out_specs=P(None, ("grp", "sub")), check_vma=False
    )
```

```python
import jax
import jax.numpy as jnp
from jax import lax
from jax.experimental import pallas as pl
from jax.experimental.pallas import tpu as pltpu
from jax.sharding import PartitionSpec as P

LEAF_GROUP = 8
NEAR_GROUP = 14
F32 = jnp.float32
BF16 = jnp.bfloat16
NT = (((1,), (1,)), ((), ()))
TN = (((0,), (0,)), ((), ()))


def dot(a, b, dims=(((1,), (0,)), ((), ()))):
    return lax.dot_general(a, b, dims, preferred_element_type=F32)


def refine_rows(payload, joined):
    span = joined.shape[0] // 4
    values = payload[:span, :].astype(F32)
    kind = payload[span : span + 1, :].astype(F32)
    spread = jnp.concatenate([jnp.where(kind == k, values, 0.0) for k in range(4)], axis=0)
    return dot(jnp.transpose(spread).astype(BF16), joined).astype(BF16)


def fetch(sources, targets, sems):
    copies = [
        pltpu.make_async_copy(source, target, sems.at[i])
        for i, (source, target) in enumerate(zip(sources, targets))
    ]
    for copy in copies:
        copy.start()
    return copies


def upward_kernel(
    dual_hbm, select_hbm, joined_hbm, p2m_hbm, m2m_hbm, payload_ref, out_ref, table_ref,
    dual, select, joined, p2m, m2m, product, refined, sems,
):
    copies = fetch(
        (dual_hbm, select_hbm, joined_hbm, p2m_hbm, m2m_hbm), (dual, select, joined, p2m, m2m), sems
    )
    subs, coarse, _ = out_ref.shape
    order, width = p2m.shape
    span, boxes = dual.shape
    out_ref[...] = jnp.zeros_like(out_ref)
    for copy in copies:
        copy.wait()
    payload_ref[:span] = dual[...]
    kind = select[...].reshape(1, boxes)
    payload_ref[span:] = jnp.broadcast_to(kind, (8, boxes)).astype(F32).astype(BF16)
    product[...] = dot(m2m[...], p2m[...])
    refined[...] = refine_rows(payload_ref[...], joined[...]).astype(F32)
    total = jnp.zeros((coarse, order), F32)
    for j in range(0, 8, 2):
        tables, rows = [], []
        for i in (j, j + 1):
            table = product[pl.ds(i, order, stride=8), :].astype(BF16)
            table_ref[:order, i * width : (i + 1) * width] = table
            tables.append(table)
            rows.append(refined[pl.ds(i, coarse, stride=8), :].astype(BF16))
        total = total + dot(jnp.concatenate(rows, axis=1), jnp.concatenate(tables, axis=1), NT)
    for d in range(subs):
        out_ref[d, :, :order] = total.astype(BF16)


class Picker:
    def __init__(self, own_ref, low_ref, high_ref, window):
        depth, self.boxes = own_ref.shape
        self.span = depth - 8
        self.window = window
        whole = jnp.concatenate(
            [low_ref[...], own_ref[...], high_ref[...], jnp.zeros((depth, 128), BF16)], axis=1
        ).astype(F32)
        self.blocks = whole.shape[1] // 256
        pieces = [whole[:, b * 256 : (b + 1) * 256] for b in range(self.blocks)]
        kinds = [piece[self.span : self.span + 1] for piece in pieces]
        kinds.append(jnp.zeros((8 - self.blocks, 256), F32))
        window[...] = jnp.concatenate([piece[: self.span] for piece in pieces] + kinds, axis=0).astype(BF16)
        self.spot = lax.broadcasted_iota(jnp.int32, (256, self.boxes), 0).astype(BF16)

    def hot(self, index):
        low = (index & 255).astype(F32).astype(BF16)
        return jnp.where(low == self.spot, jnp.array(1.0, BF16), jnp.array(0.0, BF16))

    def expand(self, index, got):
        block, span = index >> 8, self.span
        value = jnp.zeros((span, self.boxes), F32)
        kind = jnp.zeros((1, self.boxes), F32)
        for b in range(self.blocks):
            value = jnp.where(block == b, got[b * span : (b + 1) * span], value)
            kind = jnp.where(block == b, got[self.blocks * span + b : self.blocks * span + b + 1], kind)
        return [jnp.where(kind == k, value, 0.0) for k in range(4)]

    def add(self, index, table, out):
        boxes = self.boxes
        got = dot(self.window[...], jnp.concatenate([self.hot(i) for i in index], axis=1))
        parts = []
        for c, i in enumerate(index):
            parts += self.expand(i, got[:, c * boxes : (c + 1) * boxes])
        out[...] += dot(table, jnp.concatenate(parts, axis=0).astype(BF16))


def by_eights(ref, rows, classes):
    order, width = rows.shape[0] // classes, rows.shape[1]
    split = rows.reshape(order, classes // 8, 8, width)
    for b in range(classes // 8):
        ref[b, :, :width] = split[:, b].reshape(order * 8, width)


def field_kernel(
    own_ref, high_ref, low_ref, leaf_list_ref, near_list_ref, p2m_ref, m2l_ref, joined_ref, near_hbm, _,
    out_ref, near_ref, window, local, leaf_table, near_table, product, sems,
):
    copies = fetch((near_hbm,), (near_ref,), sems)
    picker = Picker(own_ref, low_ref, high_ref, window)
    order, width = p2m_ref.shape
    joined = joined_ref[...]
    classes = leaf_list_ref.shape[0]
    spread = dot(p2m_ref[...], joined, NT).astype(BF16)
    by_eights(product, dot(m2l_ref[...], spread), classes)
    for c in range(classes):
        group, at = c // LEAF_GROUP, c % LEAF_GROUP * width
        rows = product[c // 8, pl.ds(c % 8, order, stride=8), :]
        leaf_table[group, :order, at : at + width] = rows.astype(BF16)
    local[...] = jnp.zeros_like(local)
    for g in range(leaf_table.shape[0]):
        index = [leaf_list_ref[c : c + 1, :] for c in range(g * LEAF_GROUP, (g + 1) * LEAF_GROUP)]
        picker.add(index, leaf_table[g], local)
    out_ref[...] = dot(p2m_ref[...], local[:order].astype(BF16), TN)
    copies[0].wait()
    classes = near_ref.shape[0]
    for c in range(classes):
        group, at = c // NEAR_GROUP, c % NEAR_GROUP * width
        near_table[group, :, at : at + width] = dot(near_ref[c], joined, NT).astype(BF16)
    for g in range(near_table.shape[0]):
        members = range(g * NEAR_GROUP, min((g + 1) * NEAR_GROUP, classes))
        index = [near_list_ref[c : c + 1, :] for c in members]
        picker.add(index, near_table[g, :, : len(members) * width], out_ref)


def downward_kernel(
    field_ref, slab_ref, low_ref, high_ref, list_ref, payload_ref, joined_ref, table_ref, m2l_rows,
    out_ref, down, wide,
):
    order = m2l_rows.shape[1]
    classes, coarse = list_ref.shape
    by_eights(wide.at[0], m2l_rows[:, :128].astype(F32), classes)
    by_eights(wide.at[1], m2l_rows[:, 128:].astype(F32), classes)

    def class_table(c):
        rows = [wide[half, c // 8, pl.ds(c % 8, order, stride=8), :] for half in range(2)]
        return jnp.concatenate(rows, axis=1)[:, :order].astype(BF16)

    span = out_ref.shape[0]
    index = jnp.transpose(list_ref[...])
    window = jnp.concatenate([low_ref[...], slab_ref[...], high_ref[...]], axis=0)
    spot = lax.broadcasted_iota(jnp.int32, (coarse, window.shape[0]), 1)
    hot = jnp.concatenate(
        [jnp.where(index[:, c : c + 1] == spot, 1.0, 0.0).astype(BF16) for c in range(classes)], axis=0
    )
    count = hot.shape[0] // 4
    picked = jnp.concatenate(
        [dot(hot[i * count : (i + 1) * count], window).astype(BF16) for i in range(4)], axis=0
    )
    total = jnp.zeros((coarse, order), F32)
    for c in range(classes):
        total = total + dot(picked[c * coarse : (c + 1) * coarse, :order], class_table(c), NT)
    local = total.astype(BF16)
    parts = dot(local, table_ref[:order])
    for j in range(8):
        down[pl.ds(j, coarse, stride=8), :] = parts[:, j * 128 : (j + 1) * 128]
    field = (field_ref[...] + jnp.transpose(down[...])).astype(BF16)
    by_kind = dot(joined_ref[...], field)
    kind = payload_ref[span : span + 1, :].astype(F32)
    tested = jnp.zeros(out_ref.shape, F32)
    for k in range(4):
        tested = jnp.where(kind == k, by_kind[k * span : (k + 1) * span], tested)
    out_ref[...] = tested.astype(BF16)


def call(kernel, outs, scratch, args, flops, megabytes, in_hbm=(), anywhere=()):
    args = [
        pltpu.with_memory_space_constraint(x, pltpu.HBM) if i in in_hbm else x
        for i, x in enumerate(args)
    ]
    return pl.pallas_call(
        kernel,
        out_shape=outs,
        in_specs=[
            pl.BlockSpec(memory_space=pltpu.HBM if i in in_hbm else pl.ANY if i in anywhere else pltpu.VMEM)
            for i in range(len(args))
        ],
        out_specs=jax.tree.map(lambda _: pl.BlockSpec(memory_space=pltpu.VMEM), outs),
        scratch_shapes=scratch,
        compiler_params=pltpu.CompilerParams(vmem_limit_bytes=32 * 1024 * 1024),
        cost_estimate=pl.CostEstimate(
            flops=flops, bytes_accessed=int(megabytes * 1e6), transcendentals=0
        ),
    )(*args)


def shifted(block, axis, step):
    count = lax.axis_size(axis)
    return lax.ppermute(block, axis, [(i, i + step) for i in range(count) if 0 <= i + step < count])


def body(
    dual_coeffs, refine_select, refine_tiles, near_list, near_tiles, leaf_list, p2m, m2m, leaf_m2l,
    coarse_list, coarse_m2l,
):
    span, boxes = dual_coeffs.shape
    order, width = p2m.shape
    coarse = boxes // 8
    subs = lax.axis_size("sub")
    joined = jnp.transpose(refine_tiles, (0, 2, 1)).reshape(4 * span, width)
    m2m_rows = jnp.transpose(m2m, (1, 0, 2)).reshape(-1, order)
    leaf_rows = jnp.transpose(leaf_m2l, (1, 0, 2)).reshape(-1, order)
    coarse_rows = jnp.transpose(coarse_m2l, (1, 0, 2)).reshape(-1, order)
    payload, mine, table = call(
        upward_kernel,
        (
            jax.ShapeDtypeStruct((span + 8, boxes), BF16),
            jax.ShapeDtypeStruct((subs, coarse, 256), BF16),
            pltpu.HBM((176, 8 * width), BF16),
        ),
        [pltpu.VMEM(a.shape, a.dtype) for a in (dual_coeffs, refine_select, joined, p2m, m2m_rows)]
        + [
            pltpu.VMEM((8 * order, width), F32),
            pltpu.VMEM((boxes, width), F32),
            pltpu.SemaphoreType.DMA((5,)),
        ],
        (dual_coeffs, refine_select, joined, p2m, m2m_rows),
        10_000_000_000, 1.0, (0, 1, 2, 3, 4),
    )
    low = shifted(payload, ("grp", "sub"), 1)
    high = shifted(payload, ("grp", "sub"), -1)
    slab = lax.all_to_all(mine, "sub", 0, 0).reshape(subs * coarse, 256)
    windows = (payload, high, low)
    slab_low = shifted(slab, "grp", 1)
    slab_high = shifted(slab, "grp", -1)
    field = call(
        field_kernel,
        jax.ShapeDtypeStruct((width, boxes), F32),
        [
            pltpu.VMEM(near_tiles.shape, BF16),
            pltpu.VMEM((5 * span + 8, 256), BF16),
            pltpu.VMEM((176, boxes), F32),
            pltpu.VMEM((leaf_m2l.shape[0] // LEAF_GROUP, 176, LEAF_GROUP * width), BF16),
            pltpu.VMEM((-(-near_tiles.shape[0] // NEAR_GROUP), width, NEAR_GROUP * width), BF16),
            pltpu.VMEM((leaf_m2l.shape[0] // 8, 8 * order, width), F32),
            pltpu.SemaphoreType.DMA((1,)),
        ],
        (*windows, leaf_list.T, near_list.T, p2m, leaf_rows, joined, near_tiles, slab),
        2_000_000_000, 3.0, (8,), (9,),
    )
    return call(
        downward_kernel,
        jax.ShapeDtypeStruct((span, boxes), BF16),
        [
            pltpu.VMEM((boxes, width), F32),
            pltpu.VMEM((2, coarse_m2l.shape[0] // 8, 8 * order, 128), F32),
        ],
        (
            field, slab, slab_low, slab_high, coarse_list.T, payload, joined, table, coarse_rows,
        ),
        1_000_000_000, 3.0,
    )


def solution(mesh):
    placed = (
        P(None, ("grp", "sub")),
        P(("grp", "sub")),
        P(),
        P(("grp", "sub"), None),
        P(),
        P(("grp", "sub"), None),
        P(),
        P(),
        P(),
        P(("grp", "sub"), None),
        P(),
    )
    return jax.shard_map(
        body, mesh=mesh, in_specs=placed, out_specs=P(None, ("grp", "sub")), check_vma=False
    )
```

```python
import jax
import jax.numpy as jnp
from jax import lax
from jax.experimental import pallas as pl
from jax.experimental.pallas import tpu as pltpu
from jax.sharding import PartitionSpec as P

LEAF_GROUP = 16
NEAR_GROUP = 14
F32 = jnp.float32
BF16 = jnp.bfloat16
NT = (((1,), (1,)), ((), ()))
TN = (((0,), (0,)), ((), ()))


def dot(a, b, dims=(((1,), (0,)), ((), ()))):
    return lax.dot_general(a, b, dims, preferred_element_type=F32)


def refine_rows(payload, joined):
    span = joined.shape[0] // 4
    values = payload[:span, :].astype(F32)
    kind = payload[span : span + 1, :].astype(F32)
    spread = jnp.concatenate([jnp.where(kind == k, values, 0.0) for k in range(4)], axis=0)
    return dot(jnp.transpose(spread).astype(BF16), joined).astype(BF16)


def fetch(sources, targets, sems):
    copies = [
        pltpu.make_async_copy(source, target, sems.at[i])
        for i, (source, target) in enumerate(zip(sources, targets))
    ]
    for copy in copies:
        copy.start()
    return copies


def upward_kernel(
    dual_hbm, select_hbm, joined_hbm, p2m_hbm, m2m_hbm, payload_ref, out_ref, table_ref,
    dual, select, joined, p2m, m2m, product, refined, sems,
):
    copies = fetch(
        (dual_hbm, select_hbm, joined_hbm, p2m_hbm, m2m_hbm), (dual, select, joined, p2m, m2m), sems
    )
    subs, coarse, _ = out_ref.shape
    order, width = p2m.shape
    span, boxes = dual.shape
    out_ref[...] = jnp.zeros_like(out_ref)
    for copy in copies:
        copy.wait()
    payload_ref[:span] = dual[...]
    kind = select[...].reshape(1, boxes)
    payload_ref[span:] = jnp.broadcast_to(kind, (8, boxes)).astype(F32).astype(BF16)
    product[...] = dot(m2m[...], p2m[...])
    refined[...] = refine_rows(payload_ref[...], joined[...]).astype(F32)
    total = jnp.zeros((coarse, order), F32)
    for j in range(0, 8, 2):
        tables, rows = [], []
        for i in (j, j + 1):
            table = product[pl.ds(i, order, stride=8), :].astype(BF16)
            table_ref[:order, i * width : (i + 1) * width] = table
            tables.append(table)
            rows.append(refined[pl.ds(i, coarse, stride=8), :].astype(BF16))
        total = total + dot(jnp.concatenate(rows, axis=1), jnp.concatenate(tables, axis=1), NT)
    for d in range(subs):
        out_ref[d, :, :order] = total.astype(BF16)


class Picker:
    def __init__(self, own_ref, low_ref, high_ref, window):
        depth, self.boxes = own_ref.shape
        self.span = depth - 8
        self.window = window
        whole = jnp.concatenate(
            [low_ref[...], own_ref[...], high_ref[...], jnp.zeros((depth, 128), BF16)], axis=1
        ).astype(F32)
        self.blocks = whole.shape[1] // 256
        pieces = [whole[:, b * 256 : (b + 1) * 256] for b in range(self.blocks)]
        kinds = [piece[self.span : self.span + 1] for piece in pieces]
        kinds.append(jnp.zeros((8 - self.blocks, 256), F32))
        window[...] = jnp.concatenate([piece[: self.span] for piece in pieces] + kinds, axis=0).astype(BF16)
        self.spot = lax.broadcasted_iota(jnp.int32, (256, self.boxes), 0).astype(BF16)

    def hot(self, index):
        low = (index & 255).astype(F32).astype(BF16)
        return jnp.where(low == self.spot, jnp.array(1.0, BF16), jnp.array(0.0, BF16))

    def expand(self, index, got):
        block, span = index >> 8, self.span
        value = jnp.zeros((span, self.boxes), F32)
        kind = jnp.zeros((1, self.boxes), F32)
        for b in range(self.blocks):
            value = jnp.where(block == b, got[b * span : (b + 1) * span], value)
            kind = jnp.where(block == b, got[self.blocks * span + b : self.blocks * span + b + 1], kind)
        return [jnp.where(kind == k, value, 0.0) for k in range(4)]

    def add(self, index, table, out):
        boxes = self.boxes
        got = dot(self.window[...], jnp.concatenate([self.hot(i) for i in index], axis=1))
        parts = []
        for c, i in enumerate(index):
            parts += self.expand(i, got[:, c * boxes : (c + 1) * boxes])
        out[...] += dot(table, jnp.concatenate(parts, axis=0).astype(BF16))


def by_eights(ref, rows, classes):
    order, width = rows.shape[0] // classes, rows.shape[1]
    split = rows.reshape(order, classes // 8, 8, width)
    for b in range(classes // 8):
        ref[b, :, :width] = split[:, b].reshape(order * 8, width)


def field_kernel(
    own_ref, high_ref, low_ref, leaf_list_ref, near_list_ref, p2m_ref, m2l_ref, joined_ref, near_hbm, _,
    out_ref, near_ref, window, local, leaf_table, near_table, product, sems,
):
    copies = fetch((near_hbm,), (near_ref,), sems)
    picker = Picker(own_ref, low_ref, high_ref, window)
    order, width = p2m_ref.shape
    joined = joined_ref[...]
    classes = leaf_list_ref.shape[0]
    spread = dot(p2m_ref[...], joined, NT).astype(BF16)
    half = m2l_ref.shape[0] // 2
    halves = [dot(m2l_ref[i * half : (i + 1) * half], spread) for i in range(2)]
    by_eights(product, jnp.concatenate(halves, axis=0), classes)
    for c in range(classes):
        group, at = c // LEAF_GROUP, c % LEAF_GROUP * width
        rows = product[c // 8, pl.ds(c % 8, order, stride=8), :]
        leaf_table[group, :order, at : at + width] = rows.astype(BF16)
    local[...] = jnp.zeros_like(local)
    for g in range(leaf_table.shape[0]):
        index = [leaf_list_ref[c : c + 1, :] for c in range(g * LEAF_GROUP, (g + 1) * LEAF_GROUP)]
        picker.add(index, leaf_table[g], local)
    out_ref[...] = dot(p2m_ref[...], local[:order].astype(BF16), TN)
    copies[0].wait()
    classes = near_ref.shape[0]
    for c in range(classes):
        group, at = c // NEAR_GROUP, c % NEAR_GROUP * width
        near_table[group, :, at : at + width] = dot(near_ref[c], joined, NT).astype(BF16)
    for g in range(near_table.shape[0]):
        members = range(g * NEAR_GROUP, min((g + 1) * NEAR_GROUP, classes))
        index = [near_list_ref[c : c + 1, :] for c in members]
        picker.add(index, near_table[g, :, : len(members) * width], out_ref)


def downward_kernel(
    field_ref, slab_ref, low_ref, high_ref, list_ref, payload_ref, joined_ref, table_ref, m2l_rows,
    out_ref, down, wide,
):
    order = m2l_rows.shape[1]
    classes, coarse = list_ref.shape
    by_eights(wide.at[0], m2l_rows[:, :128].astype(F32), classes)
    by_eights(wide.at[1], m2l_rows[:, 128:].astype(F32), classes)

    def class_table(c):
        rows = [wide[half, c // 8, pl.ds(c % 8, order, stride=8), :] for half in range(2)]
        return jnp.concatenate(rows, axis=1)[:, :order].astype(BF16)

    span = out_ref.shape[0]
    index = jnp.transpose(list_ref[...])
    window = jnp.concatenate([low_ref[...], slab_ref[...], high_ref[...]], axis=0)
    spot = lax.broadcasted_iota(jnp.int32, (coarse, window.shape[0]), 1)
    hot = jnp.concatenate(
        [jnp.where(index[:, c : c + 1] == spot, 1.0, 0.0).astype(BF16) for c in range(classes)], axis=0
    )
    count = hot.shape[0] // 4
    picked = jnp.concatenate(
        [dot(hot[i * count : (i + 1) * count], window).astype(BF16) for i in range(4)], axis=0
    )
    total = jnp.zeros((coarse, order), F32)
    for c in range(classes):
        total = total + dot(picked[c * coarse : (c + 1) * coarse, :order], class_table(c), NT)
    local = total.astype(BF16)
    parts = dot(local, table_ref[:order])
    for j in range(8):
        down[pl.ds(j, coarse, stride=8), :] = parts[:, j * 128 : (j + 1) * 128]
    field = (field_ref[...] + jnp.transpose(down[...])).astype(BF16)
    by_kind = dot(joined_ref[...], field)
    kind = payload_ref[span : span + 1, :].astype(F32)
    tested = jnp.zeros(out_ref.shape, F32)
    for k in range(4):
        tested = jnp.where(kind == k, by_kind[k * span : (k + 1) * span], tested)
    out_ref[...] = tested.astype(BF16)


def call(kernel, outs, scratch, args, flops, megabytes, in_hbm=(), anywhere=()):
    args = [
        pltpu.with_memory_space_constraint(x, pltpu.HBM) if i in in_hbm else x
        for i, x in enumerate(args)
    ]
    return pl.pallas_call(
        kernel,
        out_shape=outs,
        in_specs=[
            pl.BlockSpec(memory_space=pltpu.HBM if i in in_hbm else pl.ANY if i in anywhere else pltpu.VMEM)
            for i in range(len(args))
        ],
        out_specs=jax.tree.map(lambda _: pl.BlockSpec(memory_space=pltpu.VMEM), outs),
        scratch_shapes=scratch,
        compiler_params=pltpu.CompilerParams(vmem_limit_bytes=32 * 1024 * 1024),
        cost_estimate=pl.CostEstimate(
            flops=flops, bytes_accessed=int(megabytes * 1e6), transcendentals=0
        ),
    )(*args)


def shifted(block, axis, step):
    count = lax.axis_size(axis)
    return lax.ppermute(block, axis, [(i, i + step) for i in range(count) if 0 <= i + step < count])


def body(
    dual_coeffs, refine_select, refine_tiles, near_list, near_tiles, leaf_list, p2m, m2m, leaf_m2l,
    coarse_list, coarse_m2l,
):
    span, boxes = dual_coeffs.shape
    order, width = p2m.shape
    coarse = boxes // 8
    subs = lax.axis_size("sub")
    joined = jnp.transpose(refine_tiles, (0, 2, 1)).reshape(4 * span, width)
    m2m_rows = jnp.transpose(m2m, (1, 0, 2)).reshape(-1, order)
    leaf_rows = jnp.transpose(leaf_m2l, (1, 0, 2)).reshape(-1, order)
    coarse_rows = jnp.transpose(coarse_m2l, (1, 0, 2)).reshape(-1, order)
    payload, mine, table = call(
        upward_kernel,
        (
            jax.ShapeDtypeStruct((span + 8, boxes), BF16),
            jax.ShapeDtypeStruct((subs, coarse, 256), BF16),
            pltpu.HBM((176, 8 * width), BF16),
        ),
        [pltpu.VMEM(a.shape, a.dtype) for a in (dual_coeffs, refine_select, joined, p2m, m2m_rows)]
        + [
            pltpu.VMEM((8 * order, width), F32),
            pltpu.VMEM((boxes, width), F32),
            pltpu.SemaphoreType.DMA((5,)),
        ],
        (dual_coeffs, refine_select, joined, p2m, m2m_rows),
        10_000_000_000, 1.0, (0, 1, 2, 3, 4),
    )
    low = shifted(payload, ("grp", "sub"), 1)
    high = shifted(payload, ("grp", "sub"), -1)
    slab = lax.all_to_all(mine, "sub", 0, 0).reshape(subs * coarse, 256)
    windows = (payload, high, low)
    slab_low = shifted(slab, "grp", 1)
    slab_high = shifted(slab, "grp", -1)
    field = call(
        field_kernel,
        jax.ShapeDtypeStruct((width, boxes), F32),
        [
            pltpu.VMEM(near_tiles.shape, BF16),
            pltpu.VMEM((5 * span + 8, 256), BF16),
            pltpu.VMEM((176, boxes), F32),
            pltpu.VMEM((leaf_m2l.shape[0] // LEAF_GROUP, 176, LEAF_GROUP * width), BF16),
            pltpu.VMEM((-(-near_tiles.shape[0] // NEAR_GROUP), width, NEAR_GROUP * width), BF16),
            pltpu.VMEM((leaf_m2l.shape[0] // 8, 8 * order, width), F32),
            pltpu.SemaphoreType.DMA((1,)),
        ],
        (*windows, leaf_list.T, near_list.T, p2m, leaf_rows, joined, near_tiles, slab),
        2_000_000_000, 3.0, (8,), (9,),
    )
    return call(
        downward_kernel,
        jax.ShapeDtypeStruct((span, boxes), BF16),
        [
            pltpu.VMEM((boxes, width), F32),
            pltpu.VMEM((2, coarse_m2l.shape[0] // 8, 8 * order, 128), F32),
        ],
        (
            field, slab, slab_low, slab_high, coarse_list.T, payload, joined, table, coarse_rows,
        ),
        1_000_000_000, 3.0,
    )


def solution(mesh):
    placed = (
        P(None, ("grp", "sub")),
        P(("grp", "sub")),
        P(),
        P(("grp", "sub"), None),
        P(),
        P(("grp", "sub"), None),
        P(),
        P(),
        P(),
        P(("grp", "sub"), None),
        P(),
    )
    return jax.shard_map(
        body, mesh=mesh, in_specs=placed, out_specs=P(None, ("grp", "sub")), check_vma=False
    )
```
